128 devices in a mesh: pos: 64 (over z, y, x), head: 2 (over core).
Axes of the slice: x: 4, y: 4, z: 4, core: 2. Of those that a mesh axis runs over, the one named last changes fastest.
Arguments:
- queries: bfloat16 [2, 8192, 4096], P(None, 'pos', 'head'), may hold values from -40 to 40
- keys_values: bfloat16 [2, 2, 8192, 512], P(None, None, 'pos', 'head'), may hold values from -10 to 10
- d_out: bfloat16 [2, 8192, 4096], P(None, 'pos', 'head'), may hold values from -6 to 6
- doc_start: int32 [8192], P('pos'), may hold values from 0 to 8191, as said below
- block_bits: int32 [512], P(('pos', 'head')), may hold values 0 or 1
Outputs:
- attended: bfloat16 [2, 8192, 4096], P(None, 'pos', 'head')
- grad_queries: bfloat16 [2, 8192, 4096], P(None, 'pos', 'head')
- grad_keys_values: bfloat16 [2, 2, 8192, 512], P(None, None, 'pos', 'head')
The draws below stay inside these ranges and needn't reach their ends.
Inputs may be any that keep to these rules, and one draw needn't show every extreme that they name: doc_start[i] is the first position of the document holding position i; documents are contiguous runs of 1 to 2048 positions, and one has exactly 2048; the last position begins a document of its own.
All inputs are finite; a program needn't handle non-finite values. No bound on the sum of `block_bits` on one device may be relied on, other than what follows from the above.
Results may differ from the reference program's by a relative error of at most 0.025.
Values may be sent and summed in bfloat16 or wider, within the bound.
No kernel may reach another device: no remote copies, remote signals or barrier semaphores. Data moves between devices by JAX's collectives and lax.ppermute only.
A program may use at most 64 MiB of HBM per device.

```python
import math
import jax
import jax.numpy as jnp
from jax import lax

BLOCK = 16
QUERY_HEADS = 32
KEY_VALUE_HEADS = 4
HEAD_SIZE = 128
LONGEST_DOC_LEN = 2048
SEQUENCE_LENGTH = 8192
NBLK = 512


def shared_draw(key):
    base_offset = jnp.clip(jax.random.normal(jax.random.fold_in(key, 11), (2, 2, SEQUENCE_LENGTH, KEY_VALUE_HEADS * HEAD_SIZE), jnp.float32), -4.0, 4.0)
    return base_offset


def draw_keys_values(key, part):
    base_offset = shared_draw(key)
    result = base_offset
    return result.astype(jnp.bfloat16)


def draw_queries(key, part):
    key = jax.random.fold_in(key, 4)
    result = jnp.clip(jax.random.normal(key, (2, SEQUENCE_LENGTH, QUERY_HEADS * HEAD_SIZE), jnp.float32), -4.0, 4.0)
    return result.astype(jnp.bfloat16)


def draw_doc_start(key, part):
    key = jax.random.fold_in(key, 5)
    place = jnp.arange(SEQUENCE_LENGTH, dtype=jnp.int32)
    shift_by = jax.random.randint(jax.random.fold_in(key, 1), (), 0, LONGEST_DOC_LEN)
    forced = place % LONGEST_DOC_LEN == shift_by
    extra = jax.random.randint(jax.random.fold_in(key, 2), (SEQUENCE_LENGTH,), 0, LONGEST_DOC_LEN) < 2
    extra = extra & jnp.logical_not((place > shift_by) & (place < shift_by + LONGEST_DOC_LEN))
    begins = forced | extra | (place == 0) | (place == SEQUENCE_LENGTH - 1)
    return lax.cummax(jnp.where(begins, place, 0), axis=0).astype(jnp.int32)


def set_ends(values, key, low, largest):
    longest = values.shape.index(max(values.shape))
    spots = []
    for shift in (0, 1):
        where = [jax.random.randint(jax.random.fold_in(key, axis), (), 0, length) for axis, length in enumerate(values.shape)]
        where[longest] = (where[longest] + shift) % values.shape[longest]
        spots.append(tuple(where))
    return values.at[spots[0]].set(low).at[spots[1]].set(largest)


def levels(key, shape, cuts, smallest, high):
    loudness, own = 1.0, jax.random.fold_in(key, 6)
    for axis_at, parts in cuts:
        heights = jnp.exp(jax.random.uniform(jax.random.fold_in(own, axis_at), (parts,), jnp.float32, smallest / len(cuts), high / len(cuts)))
        loudness = loudness * jnp.repeat(heights, shape[axis_at] // parts).reshape([-1 if axis == axis_at else 1 for axis in range(len(shape))])
    return loudness


def centred(stream_key, shape, scale, most, split=(), held_as=jnp.bfloat16):
    factor_of = levels(stream_key, shape, split, -0.22, 0.18) if split else 1.0
    array = jax.random.normal(stream_key, shape, jnp.float32) * scale * factor_of
    return jnp.minimum(jnp.maximum(array, -most), most).astype(held_as)


def setup_inputs(seed: int = 0) -> dict:
    key_list = jax.random.split(jax.random.key(seed), 6)
    return {
        "queries": draw_queries(jax.random.fold_in(key_list[5], 71), 0),
        "keys_values": draw_keys_values(jax.random.fold_in(key_list[5], 71), 0),
        "d_out": centred(key_list[2], (2, SEQUENCE_LENGTH, QUERY_HEADS * HEAD_SIZE), 1.0, 6.0, ((1, 64), (2, 2))),
        "doc_start": draw_doc_start(jax.random.fold_in(key_list[5], 71), 0),
        "block_bits": set_ends((jax.random.randint(key_list[4], (NBLK,), 0, 2) < 1).astype(jnp.int32), jax.random.fold_in(key_list[4], 1), 0, 1),
    }


def reference(queries, keys_values, d_out, doc_start, block_bits):
    query_group = QUERY_HEADS // KEY_VALUE_HEADS
    row_block = LONGEST_DOC_LEN // 4
    window_span = LONGEST_DOC_LEN + row_block
    count = SEQUENCE_LENGTH // row_block
    scale = 1.0 / math.sqrt(HEAD_SIZE)
    keep = jnp.repeat(block_bits, BLOCK).astype(jnp.bfloat16)
    output_cotangent = jnp.stack([d_out[0], d_out[1] * keep[:, None]])
    clean_pad = jnp.pad(keys_values[:, 0], ((0, 0), (LONGEST_DOC_LEN, 0), (0, 0)))
    start_pad = jnp.pad(doc_start, (LONGEST_DOC_LEN, 0), constant_values=-1)
    initial_carry = jnp.zeros((2, SEQUENCE_LENGTH + LONGEST_DOC_LEN, KEY_VALUE_HEADS * HEAD_SIZE), jnp.float32)

    def one_block(carry, index):
        first_block = (index * row_block).astype(jnp.int32)
        query_block_rows = lax.dynamic_slice_in_dim(queries, first_block, row_block, 1).astype(jnp.float32).reshape(2 * row_block, KEY_VALUE_HEADS, query_group, HEAD_SIZE)
        cotangent_rows = lax.dynamic_slice_in_dim(output_cotangent, first_block, row_block, 1).astype(jnp.float32).reshape(2 * row_block, KEY_VALUE_HEADS, query_group, HEAD_SIZE)
        nearby_block = lax.dynamic_slice_in_dim(clean_pad, first_block, window_span, 1).astype(jnp.float32)
        own_block = lax.dynamic_slice_in_dim(keys_values[:, 1], first_block, row_block, 1).astype(jnp.float32)
        key_rows = jnp.concatenate([nearby_block[0], own_block[0]], 0).reshape(window_span + row_block, KEY_VALUE_HEADS, HEAD_SIZE)
        value_rows = jnp.concatenate([nearby_block[1], own_block[1]], 0).reshape(window_span + row_block, KEY_VALUE_HEADS, HEAD_SIZE)
        q_pos = first_block + jnp.arange(row_block, dtype=jnp.int32)
        q_start = lax.dynamic_slice_in_dim(doc_start, first_block, row_block, 0)
        k_pos = jnp.concatenate([first_block - LONGEST_DOC_LEN + jnp.arange(window_span, dtype=jnp.int32), q_pos])
        k_start = jnp.concatenate([lax.dynamic_slice_in_dim(start_pad, first_block, window_span, 0), q_start])
        same = q_start[:, None] == k_start[None, :]
        q_blk = (q_pos // BLOCK)[:, None]
        k_blk = (k_pos // BLOCK)[None, :]
        clean_key = (jnp.arange(window_span + row_block, dtype=jnp.int32) < window_span)[None, :]
        see_clean = same & clean_key & (k_blk <= q_blk)
        see_noisy = same & (clean_key & (k_blk < q_blk) | jnp.logical_not(clean_key) & (k_blk == q_blk))
        allowed = jnp.concatenate([see_clean, see_noisy], 0)
        scores = jnp.einsum('rgqd,kgd->gqrk', query_block_rows, key_rows) * scale
        masked = jnp.where(allowed, scores, -1e+30)
        top = lax.optimization_barrier(jnp.max(masked, -1))
        total = lax.optimization_barrier(jnp.sum(jnp.where(allowed, jnp.exp(masked - top[..., None]), 0.0), -1))
        lse = top + jnp.log(total)
        weights = jnp.where(allowed, jnp.exp(jnp.where(allowed, scores - lse[..., None], -1e+30)), 0.0)
        weights_low = lax.optimization_barrier(weights.astype(jnp.bfloat16)).astype(jnp.float32)
        out = jnp.einsum('gqrk,kgd->rgqd', weights_low, value_rows)
        attended = out.astype(jnp.bfloat16)
        delta = lax.optimization_barrier(jnp.sum(cotangent_rows * attended.astype(jnp.float32), -1)).transpose(1, 2, 0)
        dprob = jnp.einsum('rgqd,kgd->gqrk', cotangent_rows, value_rows)
        dscore = (weights * (dprob - delta[..., None]) * scale).astype(jnp.bfloat16)
        dscore = lax.optimization_barrier(dscore).astype(jnp.float32)
        grad_q = jnp.einsum('gqrk,kgd->rgqd', dscore, key_rows).astype(jnp.bfloat16)
        key_gradient = jnp.einsum('gqrk,rgqd->kgd', dscore, query_block_rows)
        value_gradient = jnp.einsum('gqrk,rgqd->kgd', weights_low, cotangent_rows)
        gradient_terms = jnp.stack([key_gradient, value_gradient]).reshape(2, window_span + row_block, KEY_VALUE_HEADS * HEAD_SIZE)
        part = lax.dynamic_slice_in_dim(carry, first_block, window_span, 1) + gradient_terms[:, :window_span]
        carry = lax.dynamic_update_slice_in_dim(carry, part, first_block, 1)
        return (carry, (attended.reshape(2, row_block, QUERY_HEADS * HEAD_SIZE), grad_q.reshape(2, row_block, QUERY_HEADS * HEAD_SIZE), gradient_terms[:, window_span:]))
    carry, (att, gq, gradient_noisy) = lax.scan(one_block, initial_carry, jnp.arange(count, dtype=jnp.int32))
    attended = jnp.moveaxis(att, 0, 1).reshape(2, SEQUENCE_LENGTH, QUERY_HEADS * HEAD_SIZE)
    grad_queries = jnp.moveaxis(gq, 0, 1).reshape(2, SEQUENCE_LENGTH, QUERY_HEADS * HEAD_SIZE)
    noisy_gradients = jnp.moveaxis(gradient_noisy, 0, 1).reshape(2, SEQUENCE_LENGTH, KEY_VALUE_HEADS * HEAD_SIZE)
    clean_grads = carry[:, LONGEST_DOC_LEN:]
    grad_keys_values = jnp.stack([clean_grads, noisy_gradients], 1).astype(jnp.bfloat16)
    return (attended, grad_queries, grad_keys_values)
```

```python
import functools
import math

import jax
import jax.numpy as jnp
from jax import lax
from jax.experimental import pallas as pl
from jax.experimental.pallas import tpu as pltpu
from jax.sharding import Mesh
from jax.sharding import PartitionSpec as P

BLOCK = 16
QUERY_HEADS = 32
KEY_VALUE_HEADS = 4
HEAD_SIZE = 128
GROUP = QUERY_HEADS // KEY_VALUE_HEADS
REACH = 16
NEGATIVE = -1e30
SCALE = 1.0 / math.sqrt(HEAD_SIZE)
SCALE_LOG2 = SCALE * math.log2(math.e)
TILE = 256

NT = (((1,), (1,)), ((), ()))


def dot(a, b, dims=(((1,), (0,)), ((), ()))):
    return lax.dot_general(a, b, dims, preferred_element_type=jnp.float32)


def fold(x, op):
    return op(x.reshape(x.shape[0] // 8, 8, x.shape[1]), 0)


def kernel(
    rows,
    q_ref,
    do_ref,
    far_ref,
    own_ref,
    bias_ref,
    keep_ref,
    *rest,
):
    att_ref, dq_ref, back_ref, local_ref = rest[-14:-10]
    k_all, v_all, k_t, v_t, s_all, p_all, ds_all, dk_all, dv_all, unused = rest[-10:]
    step = pl.program_id(0)
    keys = k_all.shape[0]
    tiles = keys // TILE

    @pl.when(step == 0)
    def _():
        for slot in range(REACH + 2):
            at = pl.ds(slot * rows, rows)
            if slot < REACH:
                k, v = far_ref[slot, 0], far_ref[slot, 1]
            else:
                k, v = own_ref[0, slot - REACH], own_ref[1, slot - REACH]
            k_all[at, :] = k
            v_all[at, :] = v
            k_t[:, at] = k.T
            v_t[:, at] = v.T
        dk_all[...] = jnp.zeros_like(dk_all)
        dv_all[...] = jnp.zeros_like(dv_all)

    q = q_ref[...].reshape(2 * rows, HEAD_SIZE)
    top = jnp.full((8, 2 * rows), NEGATIVE, jnp.float32)
    for tile in range(tiles):
        at = pl.ds(tile * TILE, TILE)
        s = dot(k_all[at, :], q, NT) + bias_ref[at, :]
        s_all[at, :] = s
        top = jnp.maximum(top, fold(s, jnp.max))
    top = jnp.max(top, 0, keepdims=True)

    total = jnp.zeros((8, 2 * rows), jnp.float32)
    for tile in range(tiles):
        at = pl.ds(tile * TILE, TILE)
        e = jnp.exp2((s_all[at, :] - top) * SCALE_LOG2)
        s_all[at, :] = e
        p_all[at, :] = e.astype(jnp.bfloat16)
        total = total + fold(e, jnp.sum)
    inverse = 1.0 / jnp.sum(total, 0, keepdims=True)

    out_t = dot(v_t[...], p_all[...]) * inverse
    att_ref[...] = out_t.T.astype(jnp.bfloat16).reshape(2, rows, HEAD_SIZE)
    out_t = out_t.astype(jnp.bfloat16).astype(jnp.float32)
    do_t = do_ref[...].reshape(2 * rows, HEAD_SIZE).astype(jnp.float32).T
    g_t = (do_t * (inverse * keep_ref[0:1, :])).astype(jnp.bfloat16)
    delta = jnp.sum(g_t.astype(jnp.float32) * out_t, 0, keepdims=True)

    for tile in range(tiles):
        at = pl.ds(tile * TILE, TILE)
        dp = dot(v_all[at, :], g_t)
        ds_all[at, :] = (s_all[at, :] * (dp - delta)).astype(jnp.bfloat16)
    dq_t = dot(k_t[...], ds_all[...]) * SCALE
    dq_ref[...] = dq_t.T.astype(jnp.bfloat16).reshape(2, rows, HEAD_SIZE)
    for tile in range(tiles):
        at = pl.ds(tile * TILE, TILE)
        dk_all[at, :] += dot(ds_all[at, :], q)
        dv_all[at, :] += dot(p_all[at, :], g_t, NT)

    @pl.when(step == GROUP - 1)
    def _():
        for slot in range(REACH + 2):
            at = pl.ds(slot * rows, rows)
            dk = dk_all[at, :] * SCALE
            dv = dv_all[at, :]
            if slot < REACH:
                back_ref[slot, 0] = dk.astype(jnp.bfloat16)
                back_ref[slot, 1] = dv.astype(jnp.bfloat16)
            else:
                local_ref[0, slot - REACH] = dk
                local_ref[1, slot - REACH] = dv


def attend(group, queries, d_out, far, keys_values, bias, keep, earlier):
    rows = queries.shape[1]
    keys = (REACH + 2) * rows

    def column(step):
        return (0, 0, group * GROUP + step)

    by_head = pl.BlockSpec((2, rows, HEAD_SIZE), column)
    whole = lambda shape: pl.BlockSpec(shape, lambda step: (0,) * len(shape))
    hbm = pl.BlockSpec(memory_space=pl.ANY)
    far_shape = (REACH, 2, rows, HEAD_SIZE)
    local_shape = (2, 2, rows, HEAD_SIZE)
    flops = 6 * 2 * keys * 2 * rows * HEAD_SIZE * GROUP
    return pl.pallas_call(
        functools.partial(kernel, rows),
        grid=(GROUP,),
        in_specs=[
            by_head,
            by_head,
            whole(far_shape),
            pl.BlockSpec(local_shape, lambda step: (0, 0, 0, group)),
            whole((keys, 2 * rows)),
            whole((8, 2 * rows)),
        ]
        + [hbm] * len(earlier),
        out_specs=[by_head, by_head, whole(far_shape), whole(local_shape)],
        out_shape=[
            jax.ShapeDtypeStruct(queries.shape, jnp.bfloat16),
            jax.ShapeDtypeStruct(queries.shape, jnp.bfloat16),
            jax.ShapeDtypeStruct(far_shape, jnp.bfloat16),
            jax.ShapeDtypeStruct(local_shape, jnp.float32),
        ],
        scratch_shapes=[
            pltpu.VMEM((keys, HEAD_SIZE), jnp.bfloat16),
            pltpu.VMEM((keys, HEAD_SIZE), jnp.bfloat16),
            pltpu.VMEM((HEAD_SIZE, keys), jnp.bfloat16),
            pltpu.VMEM((HEAD_SIZE, keys), jnp.bfloat16),
            pltpu.VMEM((keys, 2 * rows), jnp.float32),
            pltpu.VMEM((keys, 2 * rows), jnp.bfloat16),
            pltpu.VMEM((keys, 2 * rows), jnp.bfloat16),
            pltpu.VMEM((keys, HEAD_SIZE), jnp.float32),
            pltpu.VMEM((keys, HEAD_SIZE), jnp.float32),
            pltpu.VMEM((8, 128), jnp.float32),
        ],
        input_output_aliases={6 + i: i for i in range(len(earlier))},
        compiler_params=pltpu.CompilerParams(vmem_limit_bytes=40 * 2**20),
        cost_estimate=pl.CostEstimate(
            flops=2 * flops, bytes_accessed=6 * 2**20, transcendentals=keys * 2 * rows * GROUP
        ),
        name=f"attend_{group}",
    )(queries, d_out, far, keys_values, bias, keep, *earlier)


def masks(doc_start, slab, place, places):
    rows = doc_start.shape[0]
    offset = jnp.arange(rows, dtype=jnp.int32)
    starts = jnp.concatenate([doc_start, doc_start])
    slot = jnp.arange(REACH, dtype=jnp.int32)
    base = rows * (places * slab + slot - jnp.where(slot >= place, places, 0))
    key_pos = base[:, None] + offset[None, :]
    far = key_pos[:, :, None] >= starts[None, None, :]
    same = doc_start[:, None] == starts[None, :]
    k_blk = (offset // BLOCK)[:, None]
    q_blk = jnp.concatenate([offset // BLOCK] * 2)[None, :]
    noisy = (jnp.arange(2 * rows, dtype=jnp.int32) >= rows)[None, :]
    own_clean = same & (k_blk + noisy.astype(jnp.int32) <= q_blk)
    own_noisy = same & noisy & (k_blk == q_blk)
    allowed = jnp.concatenate([far, own_clean[None], own_noisy[None]], 0)
    return jnp.where(allowed, 0.0, NEGATIVE).astype(jnp.float32).reshape(-1, 2 * rows)


def local(queries, keys_values, d_out, doc_start, block_bits):
    rows = queries.shape[1]
    slabs, places = lax.axis_size("slab"), lax.axis_size("place")
    slab, place, head = (lax.axis_index(a) for a in ("slab", "place", "head"))
    kv_heads = keys_values.shape[3] // HEAD_SIZE
    later = [(i, i + 1) for i in range(slabs - 1)]
    sooner = [(i + 1, i) for i in range(slabs - 1)]
    slot = jnp.arange(places, dtype=jnp.int32)[:, None, None, None]
    after = slot > place

    far = []
    for group in range(kv_heads):
        own = keys_values[:, 0, :, group * HEAD_SIZE : (group + 1) * HEAD_SIZE]
        before = lax.ppermute(own, "slab", later)
        send = jnp.where(after, own[None], before[None])
        far.append(lax.all_to_all(send, "place", 0, 0))

    other = lax.ppermute(block_bits, "head", [(0, 1), (1, 0)])
    bits = jnp.where(
        head == 0,
        jnp.concatenate([block_bits, other]),
        jnp.concatenate([other, block_bits]),
    )
    keep = jnp.concatenate([jnp.ones((rows,), jnp.int32), jnp.repeat(bits, BLOCK)])
    keep = jnp.broadcast_to(keep.astype(jnp.float32)[None, :], (8, 2 * rows))
    bias = masks(doc_start, slab, place, places)

    earlier = ()
    totals, noisy = [], []
    for group in range(kv_heads):
        att, dq, back, mine = attend(
            group, queries, d_out, far[group], keys_values, bias, keep, earlier
        )
        earlier = (att, dq)
        terms = lax.all_to_all(back, "place", 0, 0).astype(jnp.float32)
        here = jnp.sum(jnp.where(after, terms, 0.0), 0)
        there = jnp.sum(jnp.where(after, 0.0, terms), 0).astype(jnp.bfloat16)
        arrived = lax.ppermute(there, "slab", sooner)
        totals.append(mine[:, 0] + here + arrived.astype(jnp.float32))
        noisy.append(mine[:, 1])
    grad = jnp.stack([jnp.concatenate(totals, -1), jnp.concatenate(noisy, -1)], 1)
    return att, dq, grad.astype(jnp.bfloat16)


def solution(mesh):
    shards, heads = mesh.devices.shape
    cut = Mesh(mesh.devices.reshape(shards // REACH, REACH, heads), ("slab", "place", "head"))
    pos = ("slab", "place")
    in_specs = (
        P(None, pos, "head"),
        P(None, None, pos, "head"),
        P(None, pos, "head"),
        P(pos),
        P((*pos, "head")),
    )
    out_specs = (P(None, pos, "head"), P(None, pos, "head"), P(None, None, pos, "head"))
    return jax.shard_map(local, mesh=cut, in_specs=in_specs, out_specs=out_specs, check_vma=False)
```

```python
import functools
import math

import jax
import jax.numpy as jnp
from jax import lax
from jax.experimental import pallas as pl
from jax.experimental.pallas import tpu as pltpu
from jax.sharding import Mesh
from jax.sharding import PartitionSpec as P

BLOCK = 16
QUERY_HEADS = 32
KEY_VALUE_HEADS = 4
HEAD_SIZE = 128
GROUP = QUERY_HEADS // KEY_VALUE_HEADS
REACH = 16
NEGATIVE = -1e30
SCALE = 1.0 / math.sqrt(HEAD_SIZE)
SCALE_LOG2 = SCALE * math.log2(math.e)
TILE = 256
SLOTS = 3
VMEM_LIMIT = 60 * 2**20

NT = (((1,), (1,)), ((), ()))


def dot(a, b, dims=(((1,), (0,)), ((), ()))):
    return lax.dot_general(a, b, dims, preferred_element_type=jnp.float32)


def fold(x, op):
    return op(x.reshape(x.shape[0] // 8, 8, x.shape[1]), 0)


def kernel(
    rows,
    group,
    q_ref,
    do_ref,
    far_ref,
    own_ref,
    base_ref,
    starts_ref,
    near_ref,
    keep_ref,
    *rest,
):
    att_ref, dq_ref, back_ref, local_ref = rest[-27:-23]
    k_all, v_all, k_t, v_t, bias_all, s_all, p_all, g_all, delta_all, ds_all = rest[-23:-13]
    dk_all, dv_all, q_all, do_all, att_all, dq_all, back_all, local_all = rest[-13:-5]
    arrive, leave, arrive_far, arrive_own, leave_back = rest[-5:]
    keys = k_t.shape[1]
    per = TILE // rows
    tiles = [pl.ds(at, TILE) for at in range(0, keys, TILE)]
    own_columns = pl.ds(group * HEAD_SIZE, HEAD_SIZE)

    def tile_of(held, at):
        return held[pl.ds(at.start // rows, per)].reshape(TILE, HEAD_SIZE)

    def fetch_keys(i, held):
        return [
            pltpu.make_async_copy(far_ref.at[:, i], held.at[pl.ds(0, REACH)], arrive_far.at[i]),
            pltpu.make_async_copy(
                own_ref.at[i, :, :, own_columns], held.at[pl.ds(REACH, 2)], arrive_own.at[i]
            ),
        ]

    def send_back(at):
        slot = at.start // rows
        if slot < REACH:
            source, target = back_all.at[pl.ds(slot, per)], back_ref.at[pl.ds(slot, per)]
        else:
            source, target = local_all, local_ref
        return pltpu.make_async_copy(source, target, leave_back.at[slot // per])

    def columns(head):
        return pl.ds((group * GROUP + head) * HEAD_SIZE, HEAD_SIZE)

    def fetches(head):
        return [
            pltpu.make_async_copy(
                source.at[:, :, columns(head)], held.at[head], arrive.at[head, i]
            )
            for i, (source, held) in enumerate(((q_ref, q_all), (do_ref, do_all)))
        ]

    def send(held, target, head, i):
        return pltpu.make_async_copy(
            held.at[head], target.at[:, :, columns(head)], leave.at[head, i]
        )

    def rows_of(held, head):
        return held[head].reshape(2 * rows, HEAD_SIZE)

    def scores(head):
        for fetch in fetches(head):
            fetch.wait()
        q = rows_of(q_all, head)
        q_t = q.T
        top = jnp.full((8, 2 * rows), NEGATIVE, jnp.float32)
        for at in tiles:
            s = dot(tile_of(k_all, at), q_t) + bias_all[at, :]
            s_all[head % 2, at, :] = s
            top = jnp.maximum(top, fold(s, jnp.max))
            yield
        state[head] = jnp.max(top, 0, keepdims=True)

    def weights(head):
        top = state[head]
        total = jnp.zeros((8, 2 * rows), jnp.float32)
        for at in tiles:
            e = jnp.exp2((s_all[head % 2, at, :] - top) * SCALE_LOG2)
            p_all[head % SLOTS, at, :] = e.astype(jnp.bfloat16)
            total = total + fold(e, jnp.sum)
            yield
        state[head] = 1.0 / jnp.sum(total, 0, keepdims=True)

    def output(head):
        inverse = state[head]
        out_t = dot(v_t[...], p_all[head % SLOTS]) * inverse
        yield
        att_all[head] = out_t.T.astype(jnp.bfloat16).reshape(2, rows, HEAD_SIZE)
        send(att_all, att_ref, head, 0).start()
        yield
        out_t = out_t.astype(jnp.bfloat16).astype(jnp.float32)
        do_t = rows_of(do_all, head).astype(jnp.float32).T
        yield
        g_t = (do_t * (inverse * keep_ref[0:1, :])).astype(jnp.bfloat16)
        g_all[head % 2] = g_t
        delta = jnp.sum(g_t.astype(jnp.float32) * out_t, 0, keepdims=True)
        delta_all[head % 2] = jnp.broadcast_to(delta, (8, 2 * rows))
        yield

    def score_grads(head):
        g_t = g_all[head % 2]
        delta = delta_all[head % 2, 0:1, :]
        for at in tiles:
            dp = dot(tile_of(v_all, at), g_t)
            p = p_all[head % SLOTS, at, :].astype(jnp.float32)
            ds_all[head % 2, at, :] = (p * (dp - delta)).astype(jnp.bfloat16)
            yield

    def key_grads(head):
        q = rows_of(q_all, head)
        g = g_all[head % 2].T
        for at in tiles:
            dk = dot(ds_all[head % 2, at, :], q)
            dv = dot(p_all[head % SLOTS, at, :], g)
            if head > 0:
                dk = dk_all[at, :] + dk
                dv = dv_all[at, :] + dv
            if head < GROUP - 1:
                dk_all[at, :] = dk
                dv_all[at, :] = dv
            else:
                slot = at.start // rows
                for i, total in enumerate((dk * SCALE, dv)):
                    total = total.reshape(per, rows, HEAD_SIZE)
                    if slot < REACH:
                        back_all[pl.ds(slot, per), i] = total.astype(jnp.bfloat16)
                    else:
                        local_all[i] = total
                send_back(at).start()
            yield

    def query_grads(head):
        dq_t = dot(k_t[...], ds_all[head % 2]) * SCALE
        yield
        dq_all[head] = dq_t.T.astype(jnp.bfloat16).reshape(2, rows, HEAD_SIZE)
        send(dq_all, dq_ref, head, 1).start()
        yield

    def together(*parts):
        parts = list(parts)
        while parts:
            parts = [part for part in parts if next(part, part) is not part]

    def flip():
        for slot in range(REACH + 2):
            at = pl.ds(slot * rows, rows)
            k_t[:, at] = k_all[slot].T
            v_t[:, at] = v_all[slot].T
            if slot % per:
                yield

    for i, held in enumerate((k_all, v_all)):
        for fetch in fetch_keys(i, held):
            fetch.start()
        for fetch in fetches(i):
            fetch.start()
    for head in range(2, GROUP):
        for fetch in fetches(head):
            fetch.start()
    key = lax.broadcasted_iota(jnp.int32, (rows, 2 * rows), 0)
    starts = starts_ref[0:1, :]
    for slot in range(REACH):
        visible = key + base_ref[slot] >= starts
        bias_all[pl.ds(slot * rows, rows), :] = jnp.where(visible, 0.0, NEGATIVE)
    bias_all[pl.ds(REACH * rows, 2 * rows), :] = near_ref[...]
    for i, held in enumerate((k_all, v_all)):
        for fetch in fetch_keys(i, held):
            fetch.wait()

    state = {}
    for turn in range(-3, GROUP):
        ready = lambda head: 0 <= head < GROUP
        parts = []
        if ready(turn + 1):
            parts.append(output(turn + 1))
        if ready(turn):
            parts.append(score_grads(turn))
        if ready(turn + 3):
            parts.append(scores(turn + 3))
        if ready(turn - 1):
            parts.append(query_grads(turn - 1))
        if turn == -3:
            parts.append(flip())
        together(*parts)
        parts = []
        if ready(turn):
            parts.append(key_grads(turn))
        if ready(turn + 2):
            parts.append(weights(turn + 2))
        together(*parts)
    together(query_grads(GROUP - 1))

    for at in tiles:
        send_back(at).wait()
    for head in range(GROUP):
        send(att_all, att_ref, head, 0).wait()
        send(dq_all, dq_ref, head, 1).wait()


def attend(group, queries, d_out, far, keys_values, base, starts, near, keep, earlier):
    rows = queries.shape[1]
    keys = (REACH + 2) * rows
    whole = lambda shape: pl.BlockSpec(shape, lambda step: (0,) * len(shape))
    hbm = pl.BlockSpec(memory_space=pltpu.HBM)
    far_shape = (REACH, 2, rows, HEAD_SIZE)
    local_shape = (2, 2, rows, HEAD_SIZE)
    held = pltpu.VMEM((GROUP, 2, rows, HEAD_SIZE), jnp.bfloat16)
    flops = 6 * 2 * keys * 2 * rows * HEAD_SIZE * GROUP
    return pl.pallas_call(
        functools.partial(kernel, rows, group),
        grid=(1,),
        in_specs=[
            hbm,
            hbm,
            hbm,
            hbm,
            pl.BlockSpec(memory_space=pltpu.SMEM),
            whole((8, 2 * rows)),
            whole((2 * rows, 2 * rows)),
            whole((8, 2 * rows)),
        ]
        + [hbm] * len(earlier),
        out_specs=[hbm, hbm, hbm, hbm],
        out_shape=[
            jax.ShapeDtypeStruct(queries.shape, jnp.bfloat16),
            jax.ShapeDtypeStruct(queries.shape, jnp.bfloat16),
            jax.ShapeDtypeStruct(far_shape, jnp.bfloat16),
            jax.ShapeDtypeStruct(local_shape, jnp.float32),
        ],
        scratch_shapes=[
            pltpu.VMEM((REACH + 2, rows, HEAD_SIZE), jnp.bfloat16),
            pltpu.VMEM((REACH + 2, rows, HEAD_SIZE), jnp.bfloat16),
            pltpu.VMEM((HEAD_SIZE, keys), jnp.bfloat16),
            pltpu.VMEM((HEAD_SIZE, keys), jnp.bfloat16),
            pltpu.VMEM((keys, 2 * rows), jnp.float32),
            pltpu.VMEM((2, keys, 2 * rows), jnp.float32),
            pltpu.VMEM((SLOTS, keys, 2 * rows), jnp.bfloat16),
            pltpu.VMEM((2, HEAD_SIZE, 2 * rows), jnp.bfloat16),
            pltpu.VMEM((2, 8, 2 * rows), jnp.float32),
            pltpu.VMEM((2, keys, 2 * rows), jnp.bfloat16),
            pltpu.VMEM((keys, HEAD_SIZE), jnp.float32),
            pltpu.VMEM((keys, HEAD_SIZE), jnp.float32),
            held,
            held,
            held,
            held,
            pltpu.VMEM(far_shape, jnp.bfloat16),
            pltpu.VMEM(local_shape, jnp.float32),
            pltpu.SemaphoreType.DMA((GROUP, 2)),
            pltpu.SemaphoreType.DMA((GROUP, 2)),
            pltpu.SemaphoreType.DMA((2,)),
            pltpu.SemaphoreType.DMA((2,)),
            pltpu.SemaphoreType.DMA((keys // TILE,)),
        ],
        input_output_aliases={8 + i: i for i in range(len(earlier))},
        compiler_params=pltpu.CompilerParams(vmem_limit_bytes=VMEM_LIMIT),
        cost_estimate=pl.CostEstimate(
            flops=2 * flops, bytes_accessed=6 * 2**20, transcendentals=keys * 2 * rows * GROUP
        ),
        name=f"attend_{group}",
    )(queries, d_out, far, keys_values, base, starts, near, keep, *earlier)


def masks(doc_start, slab, place, places):
    rows = doc_start.shape[0]
    offset = jnp.arange(rows, dtype=jnp.int32)
    starts = jnp.concatenate([doc_start, doc_start])[None, :]
    slot = jnp.arange(REACH, dtype=jnp.int32)
    base = rows * (places * slab + slot - jnp.where(slot >= place, places, 0))
    same = doc_start[:, None] == starts
    k_blk = (offset // BLOCK)[:, None]
    q_blk = jnp.concatenate([offset // BLOCK] * 2)[None, :]
    noisy = (jnp.arange(2 * rows, dtype=jnp.int32) >= rows)[None, :]
    own_clean = same & (k_blk + noisy.astype(jnp.int32) <= q_blk)
    own_noisy = same & noisy & (k_blk == q_blk)
    near = jnp.where(jnp.concatenate([own_clean, own_noisy], 0), 0.0, NEGATIVE)
    return base, jnp.broadcast_to(starts, (8, 2 * rows)), near.astype(jnp.float32)


def local(queries, keys_values, d_out, doc_start, block_bits):
    rows = queries.shape[1]
    slabs, places = lax.axis_size("slab"), lax.axis_size("place")
    slab, place, head = (lax.axis_index(a) for a in ("slab", "place", "head"))
    kv_heads = keys_values.shape[3] // HEAD_SIZE
    later = [(i, i + 1) for i in range(slabs - 1)]
    sooner = [(i + 1, i) for i in range(slabs - 1)]
    slot = jnp.arange(places, dtype=jnp.int32)[:, None, None, None]
    after = slot > place

    own = keys_values[:, 0]
    before = lax.ppermute(own, "slab", later)
    far = []
    for group in range(kv_heads):
        part = slice(group * HEAD_SIZE, (group + 1) * HEAD_SIZE)
        send = jnp.where(after, own[None, :, :, part], before[None, :, :, part])
        far.append(lax.all_to_all(send, "place", 0, 0))

    other = lax.ppermute(block_bits, "head", [(0, 1), (1, 0)])
    bits = jnp.where(
        head == 0,
        jnp.concatenate([block_bits, other]),
        jnp.concatenate([other, block_bits]),
    )
    keep = jnp.concatenate([jnp.ones((rows,), jnp.int32), jnp.repeat(bits, BLOCK)])
    keep = jnp.broadcast_to(keep.astype(jnp.float32)[None, :], (8, 2 * rows))
    base, starts, near = masks(doc_start, slab, place, places)

    earlier = ()
    totals, noisy = [], []
    for group in range(kv_heads):
        att, dq, back, mine = attend(
            group, queries, d_out, far[group], keys_values, base, starts, near, keep, earlier
        )
        earlier = (att, dq)
        if totals:
            back, totals[-1] = lax.optimization_barrier((back, totals[-1]))
        terms = lax.all_to_all(back, "place", 0, 0)
        totals.append(terms)
        noisy.append(mine)
    for group, (terms, mine) in enumerate(zip(totals, noisy)):
        terms = terms.astype(jnp.float32)
        here = jnp.sum(jnp.where(after, terms, 0.0), 0)
        there = jnp.sum(jnp.where(after, 0.0, terms), 0).astype(jnp.bfloat16)
        arrived = lax.ppermute(there, "slab", sooner)
        totals[group] = mine[:, 0] + here + arrived.astype(jnp.float32)
        noisy[group] = mine[:, 1]
    grad = jnp.stack([jnp.concatenate(totals, -1), jnp.concatenate(noisy, -1)], 1)
    return att, dq, grad.astype(jnp.bfloat16)


def solution(mesh):
    shards, heads = mesh.devices.shape
    cut = Mesh(mesh.devices.reshape(shards // REACH, REACH, heads), ("slab", "place", "head"))
    pos = ("slab", "place")
    in_specs = (
        P(None, pos, "head"),
        P(None, None, pos, "head"),
        P(None, pos, "head"),
        P(pos),
        P((*pos, "head")),
    )
    out_specs = (P(None, pos, "head"), P(None, pos, "head"), P(None, None, pos, "head"))
    return jax.shard_map(local, mesh=cut, in_specs=in_specs, out_specs=out_specs, check_vma=False)
```

```python
import functools
import math

import jax
import jax.numpy as jnp
from jax import lax
from jax.experimental import pallas as pl
from jax.experimental.pallas import tpu as pltpu
from jax.sharding import Mesh
from jax.sharding import PartitionSpec as P

BLOCK = 16
QUERY_HEADS = 32
KEY_VALUE_HEADS = 4
HEAD_SIZE = 128
GROUP = QUERY_HEADS // KEY_VALUE_HEADS
REACH = 16
NEGATIVE = -1e30
SCALE = 1.0 / math.sqrt(HEAD_SIZE)
SCALE_LOG2 = SCALE * math.log2(math.e)
TILE = 256
SLOTS = 3
VMEM_LIMIT = 50 * 2**20

NT = (((1,), (1,)), ((), ()))


def dot(a, b, dims=(((1,), (0,)), ((), ()))):
    return lax.dot_general(a, b, dims, preferred_element_type=jnp.float32)


def fold(x, op):
    return op(x.reshape(x.shape[0] // 8, 8, x.shape[1]), 0)


def kernel(
    rows,
    group,
    q_ref,
    do_ref,
    far_ref,
    own_ref,
    base_ref,
    starts_ref,
    near_ref,
    keep_ref,
    *rest,
):
    att_ref, dq_ref, back_ref, local_ref = rest[-27:-23]
    k_all, v_all, k_t, v_t, bias_all, s_all, p_all, g_all, delta_all, ds_all = rest[-23:-13]
    dk_all, dv_all, q_all, do_all, att_all, dq_all, back_all, local_all = rest[-13:-5]
    arrive, leave, arrive_far, arrive_own, leave_back = rest[-5:]
    keys = k_t.shape[1]
    per = TILE // rows
    tiles = [pl.ds(at, TILE) for at in range(0, keys, TILE)]
    own_columns = pl.ds(group * HEAD_SIZE, HEAD_SIZE)

    def tile_of(held, at):
        return held[pl.ds(at.start // rows, per)].reshape(TILE, HEAD_SIZE)

    def fetch_keys(i, held):
        return [
            pltpu.make_async_copy(far_ref.at[:, i], held.at[pl.ds(0, REACH)], arrive_far.at[i]),
            pltpu.make_async_copy(
                own_ref.at[i, :, :, own_columns], held.at[pl.ds(REACH, 2)], arrive_own.at[i]
            ),
        ]

    def send_back(at):
        slot = at.start // rows
        if slot < REACH:
            source, target = back_all.at[pl.ds(slot, per)], back_ref.at[pl.ds(slot, per)]
        else:
            source, target = local_all, local_ref
        return pltpu.make_async_copy(source, target, leave_back.at[slot // per])

    def columns(head):
        return pl.ds((group * GROUP + head) * HEAD_SIZE, HEAD_SIZE)

    def fetches(head):
        return [
            pltpu.make_async_copy(
                source.at[:, :, columns(head)], held.at[head], arrive.at[head, i]
            )
            for i, (source, held) in enumerate(((q_ref, q_all), (do_ref, do_all)))
        ]

    def send(held, target, head, i):
        return pltpu.make_async_copy(
            held.at[head], target.at[:, :, columns(head)], leave.at[head, i]
        )

    def rows_of(held, head):
        return held[head].reshape(2 * rows, HEAD_SIZE)

    def scores(head):
        for fetch in fetches(head):
            fetch.wait()
        q = rows_of(q_all, head)
        q_t = q.T
        top = jnp.full((8, 2 * rows), NEGATIVE, jnp.float32)
        for at in tiles:
            s = dot(tile_of(k_all, at), q_t) + bias_all[at, :]
            s_all[head % 2, at, :] = s
            top = jnp.maximum(top, fold(s, jnp.max))
            yield
        state[head] = jnp.max(top, 0, keepdims=True)

    def weights(head):
        top = state[head]
        total = jnp.zeros((8, 2 * rows), jnp.float32)
        for at in tiles:
            e = jnp.exp2((s_all[head % 2, at, :] - top) * SCALE_LOG2)
            p_all[head % SLOTS, at, :] = e.astype(jnp.bfloat16)
            total = total + fold(e, jnp.sum)
            yield
        state[head] = 1.0 / jnp.sum(total, 0, keepdims=True)

    def output(head):
        inverse = state[head]
        out_t = dot(v_t[...], p_all[head % SLOTS]) * inverse
        yield
        att_all[head] = out_t.T.astype(jnp.bfloat16).reshape(2, rows, HEAD_SIZE)
        send(att_all, att_ref, head, 0).start()
        yield
        out_t = out_t.astype(jnp.bfloat16).astype(jnp.float32)
        do_t = rows_of(do_all, head).astype(jnp.float32).T
        yield
        g_t = (do_t * (inverse * keep_ref[...])).astype(jnp.bfloat16)
        g_all[head % 2] = g_t
        delta = jnp.sum(g_t.astype(jnp.float32) * out_t, 0, keepdims=True)
        delta_all[head % 2] = jnp.broadcast_to(delta, (8, 2 * rows))
        yield

    def score_grads(head):
        g_t = g_all[head % 2]
        delta = delta_all[head % 2, 0:1, :]
        for at in tiles:
            dp = dot(tile_of(v_all, at), g_t)
            p = p_all[head % SLOTS, at, :].astype(jnp.float32)
            ds_all[head % 2, at, :] = (p * (dp - delta)).astype(jnp.bfloat16)
            yield

    def key_grads(head):
        q = rows_of(q_all, head)
        g = g_all[head % 2].T
        for at in tiles:
            dk = dot(ds_all[head % 2, at, :], q)
            dv = dot(p_all[head % SLOTS, at, :], g)
            if head > 0:
                dk = dk_all[at, :] + dk
                dv = dv_all[at, :] + dv
            if head < GROUP - 1:
                dk_all[at, :] = dk
                dv_all[at, :] = dv
            else:
                slot = at.start // rows
                for i, total in enumerate((dk * SCALE, dv)):
                    total = total.reshape(per, rows, HEAD_SIZE)
                    if slot < REACH:
                        back_all[pl.ds(slot, per), i] = total.astype(jnp.bfloat16)
                    else:
                        local_all[i] = total
                send_back(at).start()
            yield

    def query_grads(head):
        dq_t = dot(k_t[...], ds_all[head % 2]) * SCALE
        yield
        dq_all[head] = dq_t.T.astype(jnp.bfloat16).reshape(2, rows, HEAD_SIZE)
        send(dq_all, dq_ref, head, 1).start()
        yield

    def together(*parts):
        parts = list(parts)
        while parts:
            parts = [part for part in parts if next(part, part) is not part]

    def flip():
        for slot in range(REACH + 2):
            at = pl.ds(slot * rows, rows)
            k_t[:, at] = k_all[slot].T
            v_t[:, at] = v_all[slot].T
            if slot % per:
                yield

    for i, held in enumerate((k_all, v_all)):
        for fetch in fetch_keys(i, held):
            fetch.start()
        for fetch in fetches(i):
            fetch.start()
    for head in range(2, GROUP):
        for fetch in fetches(head):
            fetch.start()
    key = lax.broadcasted_iota(jnp.int32, (rows, 2 * rows), 0)
    starts = starts_ref[...]
    for slot in range(REACH):
        visible = key + base_ref[slot] >= starts
        bias_all[pl.ds(slot * rows, rows), :] = jnp.where(visible, 0.0, NEGATIVE)
    bias_all[pl.ds(REACH * rows, 2 * rows), :] = near_ref[...]
    for i, held in enumerate((k_all, v_all)):
        for fetch in fetch_keys(i, held):
            fetch.wait()

    state = {}
    for turn in range(-3, GROUP):
        ready = lambda head: 0 <= head < GROUP
        parts = []
        if ready(turn + 1):
            parts.append(output(turn + 1))
        if ready(turn):
            parts.append(score_grads(turn))
        if ready(turn + 3):
            parts.append(scores(turn + 3))
        if ready(turn - 1):
            parts.append(query_grads(turn - 1))
        if turn == -3:
            parts.append(flip())
        together(*parts)
        parts = []
        if ready(turn):
            parts.append(key_grads(turn))
        if ready(turn + 2):
            parts.append(weights(turn + 2))
        together(*parts)
    together(query_grads(GROUP - 1))

    for at in tiles:
        send_back(at).wait()
    for head in range(GROUP):
        send(att_all, att_ref, head, 0).wait()
        send(dq_all, dq_ref, head, 1).wait()


def attend(group, queries, d_out, far, keys_values, base, starts, near, keep, earlier):
    rows = queries.shape[1]
    keys = (REACH + 2) * rows
    whole = lambda shape: pl.BlockSpec(shape, lambda step: (0,) * len(shape))
    hbm = pl.BlockSpec(memory_space=pl.ANY)
    far_shape = (REACH, 2, rows, HEAD_SIZE)
    local_shape = (2, 2, rows, HEAD_SIZE)
    held = pltpu.VMEM((GROUP, 2, rows, HEAD_SIZE), jnp.bfloat16)
    flops = 6 * 2 * keys * 2 * rows * HEAD_SIZE * GROUP
    return pl.pallas_call(
        functools.partial(kernel, rows, group),
        grid=(1,),
        in_specs=[
            hbm,
            hbm,
            hbm,
            hbm,
            pl.BlockSpec(memory_space=pltpu.SMEM),
            whole((1, 2 * rows)),
            whole((2 * rows, 2 * rows)),
            whole((1, 2 * rows)),
        ]
        + [hbm] * len(earlier),
        out_specs=[hbm, hbm, hbm, hbm],
        out_shape=[
            jax.ShapeDtypeStruct(queries.shape, jnp.bfloat16),
            jax.ShapeDtypeStruct(queries.shape, jnp.bfloat16),
            jax.ShapeDtypeStruct(far_shape, jnp.bfloat16),
            jax.ShapeDtypeStruct(local_shape, jnp.float32),
        ],
        scratch_shapes=[
            pltpu.VMEM((REACH + 2, rows, HEAD_SIZE), jnp.bfloat16),
            pltpu.VMEM((REACH + 2, rows, HEAD_SIZE), jnp.bfloat16),
            pltpu.VMEM((HEAD_SIZE, keys), jnp.bfloat16),
            pltpu.VMEM((HEAD_SIZE, keys), jnp.bfloat16),
            pltpu.VMEM((keys, 2 * rows), jnp.float32),
            pltpu.VMEM((2, keys, 2 * rows), jnp.float32),
            pltpu.VMEM((SLOTS, keys, 2 * rows), jnp.bfloat16),
            pltpu.VMEM((2, HEAD_SIZE, 2 * rows), jnp.bfloat16),
            pltpu.VMEM((2, 8, 2 * rows), jnp.float32),
            pltpu.VMEM((2, keys, 2 * rows), jnp.bfloat16),
            pltpu.VMEM((keys, HEAD_SIZE), jnp.float32),
            pltpu.VMEM((keys, HEAD_SIZE), jnp.float32),
            held,
            held,
            held,
            held,
            pltpu.VMEM(far_shape, jnp.bfloat16),
            pltpu.VMEM(local_shape, jnp.float32),
            pltpu.SemaphoreType.DMA((GROUP, 2)),
            pltpu.SemaphoreType.DMA((GROUP, 2)),
            pltpu.SemaphoreType.DMA((2,)),
            pltpu.SemaphoreType.DMA((2,)),
            pltpu.SemaphoreType.DMA((keys // TILE,)),
        ],
        input_output_aliases={8 + i: i for i in range(len(earlier))},
        compiler_params=pltpu.CompilerParams(vmem_limit_bytes=VMEM_LIMIT),
        cost_estimate=pl.CostEstimate(
            flops=2 * flops, bytes_accessed=6 * 2**20, transcendentals=keys * 2 * rows * GROUP
        ),
        name=f"attend_{group}",
    )(queries, d_out, far, keys_values, base, starts, near, keep, *earlier)


def masks(doc_start, slab, place, places):
    rows = doc_start.shape[0]
    offset = jnp.arange(rows, dtype=jnp.int32)
    starts = jnp.concatenate([doc_start, doc_start])[None, :]
    slot = jnp.arange(REACH, dtype=jnp.int32)
    base = rows * (places * slab + slot - jnp.where(slot >= place, places, 0))
    same = doc_start[:, None] == starts
    k_blk = (offset // BLOCK)[:, None]
    q_blk = jnp.concatenate([offset // BLOCK] * 2)[None, :]
    noisy = (jnp.arange(2 * rows, dtype=jnp.int32) >= rows)[None, :]
    own_clean = same & (k_blk + noisy.astype(jnp.int32) <= q_blk)
    own_noisy = same & noisy & (k_blk == q_blk)
    near = jnp.where(jnp.concatenate([own_clean, own_noisy], 0), 0.0, NEGATIVE)
    return base, starts, near.astype(jnp.float32)


def local(queries, keys_values, d_out, doc_start, block_bits):
    rows = queries.shape[1]
    slabs, places = lax.axis_size("slab"), lax.axis_size("place")
    slab, place, head = (lax.axis_index(a) for a in ("slab", "place", "head"))
    kv_heads = keys_values.shape[3] // HEAD_SIZE
    later = [(i, i + 1) for i in range(slabs - 1)]
    sooner = [(i + 1, i) for i in range(slabs - 1)]
    slot = jnp.arange(places, dtype=jnp.int32)[:, None, None, None]
    after = slot > place

    own = keys_values[:, 0]
    before = lax.ppermute(own, "slab", later)
    far = []
    for group in range(kv_heads):
        part = slice(group * HEAD_SIZE, (group + 1) * HEAD_SIZE)
        send = jnp.where(after, own[None, :, :, part], before[None, :, :, part])
        far.append(lax.all_to_all(send, "place", 0, 0))

    other = lax.ppermute(block_bits, "head", [(0, 1), (1, 0)])
    bits = jnp.where(
        head == 0,
        jnp.concatenate([block_bits, other]),
        jnp.concatenate([other, block_bits]),
    )
    keep = jnp.concatenate([jnp.ones((rows,), jnp.int32), jnp.repeat(bits, BLOCK)])
    keep = keep.astype(jnp.float32)[None, :]
    base, starts, near = masks(doc_start, slab, place, places)

    earlier = ()
    totals, noisy = [], []
    for group in range(kv_heads):
        att, dq, back, mine = attend(
            group, queries, d_out, far[group], keys_values, base, starts, near, keep, earlier
        )
        earlier = (att, dq)
        if totals:
            back, totals[-1] = lax.optimization_barrier((back, totals[-1]))
        terms = lax.all_to_all(back, "place", 0, 0)
        totals.append(terms)
        noisy.append(mine)
    here, there = [], []
    for terms in totals:
        terms = terms.astype(jnp.float32)
        here.append(jnp.sum(jnp.where(after, terms, 0.0), 0))
        there.append(jnp.sum(jnp.where(after, 0.0, terms), 0).astype(jnp.bfloat16))
    arrived = lax.ppermute(jnp.concatenate(there, -1), "slab", sooner)
    clean = jnp.concatenate([a + b[:, 0] for a, b in zip(here, noisy)], -1)
    clean = clean + arrived.astype(jnp.float32)
    grad = jnp.stack([clean, jnp.concatenate([b[:, 1] for b in noisy], -1)], 1)
    return att, dq, grad.astype(jnp.bfloat16)


def solution(mesh):
    shards, heads = mesh.devices.shape
    cut = Mesh(mesh.devices.reshape(shards // REACH, REACH, heads), ("slab", "place", "head"))
    pos = ("slab", "place")
    in_specs = (
        P(None, pos, "head"),
        P(None, None, pos, "head"),
        P(None, pos, "head"),
        P(pos),
        P((*pos, "head")),
    )
    out_specs = (P(None, pos, "head"), P(None, pos, "head"), P(None, None, pos, "head"))
    return jax.shard_map(local, mesh=cut, in_specs=in_specs, out_specs=out_specs, check_vma=False)
```

```python
import functools
import math

import jax
import jax.numpy as jnp
from jax import lax
from jax.experimental import pallas as pl
from jax.experimental.pallas import tpu as pltpu
from jax.sharding import Mesh
from jax.sharding import PartitionSpec as P

BLOCK = 16
QUERY_HEADS = 32
KEY_VALUE_HEADS = 4
HEAD_SIZE = 128
GROUP = QUERY_HEADS // KEY_VALUE_HEADS
REACH = 16
NEGATIVE = -1e30
SCALE = 1.0 / math.sqrt(HEAD_SIZE)
SCALE_LOG2 = SCALE * math.log2(math.e)
TILE = 256
SLOTS = 3
VMEM_LIMIT = 50 * 2**20

NT = (((1,), (1,)), ((), ()))


def dot(a, b, dims=(((1,), (0,)), ((), ()))):
    return lax.dot_general(a, b, dims, preferred_element_type=jnp.float32)


def fold(x, op):
    return op(x.reshape(x.shape[0] // 8, 8, x.shape[1]), 0)


def kernel(
    rows,
    group,
    q_ref,
    do_ref,
    far_ref,
    own_ref,
    base_ref,
    which_ref,
    starts_ref,
    near_ref,
    keep_ref,
    *rest,
):
    att_ref, dq_ref, back_ref, local_ref = rest[-27:-23]
    k_all, v_all, k_t, v_t, bias_all, s_all, p_all, g_all, delta_all, ds_all = rest[-23:-13]
    dk_all, dv_all, q_all, do_all, att_all, dq_all, back_all, local_all = rest[-13:-5]
    arrive, leave, arrive_far, arrive_own, leave_back = rest[-5:]
    keys = k_t.shape[1]
    per = TILE // rows
    tiles = [pl.ds(at, TILE) for at in range(0, keys, TILE)]
    own_columns = pl.ds(group * HEAD_SIZE, HEAD_SIZE)

    def tile_of(held, at):
        return held[pl.ds(at.start // rows, per)].reshape(TILE, HEAD_SIZE)

    def fetch_keys(i, held):
        if len(far_ref.shape) == 4:
            far = [(far_ref.at[:, i], held.at[pl.ds(0, REACH)], arrive_far.at[i, 0])]
        else:
            far = [
                (far_ref.at[slot, which_ref[slot], i], held.at[slot], arrive_far.at[i, slot])
                for slot in range(REACH)
            ]
        return [pltpu.make_async_copy(*one) for one in far] + [
            pltpu.make_async_copy(
                own_ref.at[i, :, :, own_columns], held.at[pl.ds(REACH, 2)], arrive_own.at[i]
            ),
        ]

    def send_back(at):
        slot = at.start // rows
        if slot < REACH:
            source, target = back_all.at[pl.ds(slot, per)], back_ref.at[pl.ds(slot, per)]
        else:
            source, target = local_all, local_ref
        return pltpu.make_async_copy(source, target, leave_back.at[slot // per])

    def columns(head):
        return pl.ds((group * GROUP + head) * HEAD_SIZE, HEAD_SIZE)

    def fetches(head):
        return [
            pltpu.make_async_copy(
                source.at[:, :, columns(head)], held.at[head], arrive.at[head, i]
            )
            for i, (source, held) in enumerate(((q_ref, q_all), (do_ref, do_all)))
        ]

    def send(held, target, head, i):
        return pltpu.make_async_copy(
            held.at[head], target.at[:, :, columns(head)], leave.at[head, i]
        )

    def rows_of(held, head):
        return held[head].reshape(2 * rows, HEAD_SIZE)

    def scores(head):
        for fetch in fetches(head):
            fetch.wait()
        q = rows_of(q_all, head)
        q_t = q.T
        top = jnp.full((8, 2 * rows), NEGATIVE, jnp.float32)
        for at in tiles:
            s = dot(tile_of(k_all, at), q_t) + bias_all[at, :]
            s_all[head % 2, at, :] = s
            top = jnp.maximum(top, fold(s, jnp.max))
            yield
        state[head] = jnp.max(top, 0, keepdims=True)

    def weights(head):
        top = state[head]
        total = jnp.zeros((8, 2 * rows), jnp.float32)
        for at in tiles:
            e = jnp.exp2((s_all[head % 2, at, :] - top) * SCALE_LOG2)
            p_all[head % SLOTS, at, :] = e.astype(jnp.bfloat16)
            total = total + fold(e, jnp.sum)
            yield
        state[head] = 1.0 / jnp.sum(total, 0, keepdims=True)

    def output(head):
        inverse = state[head]
        out_t = dot(v_t[...], p_all[head % SLOTS]) * inverse
        yield
        att_all[head] = out_t.T.astype(jnp.bfloat16).reshape(2, rows, HEAD_SIZE)
        send(att_all, att_ref, head, 0).start()
        yield
        out_t = out_t.astype(jnp.bfloat16).astype(jnp.float32)
        do_t = rows_of(do_all, head).astype(jnp.float32).T
        yield
        g_t = (do_t * (inverse * keep_ref[...])).astype(jnp.bfloat16)
        g_all[head % 2] = g_t
        delta = jnp.sum(g_t.astype(jnp.float32) * out_t, 0, keepdims=True)
        delta_all[head % 2] = jnp.broadcast_to(delta, (8, 2 * rows))
        yield

    def score_grads(head):
        g_t = g_all[head % 2]
        delta = delta_all[head % 2, 0:1, :]
        for at in tiles:
            dp = dot(tile_of(v_all, at), g_t)
            p = p_all[head % SLOTS, at, :].astype(jnp.float32)
            ds_all[head % 2, at, :] = (p * (dp - delta)).astype(jnp.bfloat16)
            yield

    def key_grads(head):
        q = rows_of(q_all, head)
        g = g_all[head % 2].T
        for at in tiles:
            dk = dot(ds_all[head % 2, at, :], q)
            dv = dot(p_all[head % SLOTS, at, :], g)
            if head > 0:
                dk = dk_all[at, :] + dk
                dv = dv_all[at, :] + dv
            if head < GROUP - 1:
                dk_all[at, :] = dk
                dv_all[at, :] = dv
            else:
                slot = at.start // rows
                for i, total in enumerate((dk * SCALE, dv)):
                    total = total.reshape(per, rows, HEAD_SIZE)
                    if slot < REACH:
                        back_all[pl.ds(slot, per), i] = total.astype(jnp.bfloat16)
                    else:
                        local_all[i] = total
                send_back(at).start()
            yield

    def query_grads(head):
        dq_t = dot(k_t[...], ds_all[head % 2]) * SCALE
        yield
        dq_all[head] = dq_t.T.astype(jnp.bfloat16).reshape(2, rows, HEAD_SIZE)
        send(dq_all, dq_ref, head, 1).start()
        yield

    def together(*parts):
        parts = list(parts)
        while parts:
            parts = [part for part in parts if next(part, part) is not part]

    def flip():
        for slot in range(REACH + 2):
            at = pl.ds(slot * rows, rows)
            k_t[:, at] = k_all[slot].T
            v_t[:, at] = v_all[slot].T
            if slot % per:
                yield

    for i, held in enumerate((k_all, v_all)):
        for fetch in fetch_keys(i, held):
            fetch.start()
        for fetch in fetches(i):
            fetch.start()
    for head in range(2, GROUP):
        for fetch in fetches(head):
            fetch.start()
    key = lax.broadcasted_iota(jnp.int32, (rows, 2 * rows), 0)
    starts = starts_ref[...]
    for slot in range(REACH):
        visible = key + base_ref[slot] >= starts
        bias_all[pl.ds(slot * rows, rows), :] = jnp.where(visible, 0.0, NEGATIVE)
    bias_all[pl.ds(REACH * rows, 2 * rows), :] = near_ref[...]
    for i, held in enumerate((k_all, v_all)):
        for fetch in fetch_keys(i, held):
            fetch.wait()

    state = {}
    for turn in range(-3, GROUP):
        ready = lambda head: 0 <= head < GROUP
        parts = []
        if ready(turn + 1):
            parts.append(output(turn + 1))
        if ready(turn):
            parts.append(score_grads(turn))
        if ready(turn + 3):
            parts.append(scores(turn + 3))
        if ready(turn - 1):
            parts.append(query_grads(turn - 1))
        if turn == -3:
            parts.append(flip())
        together(*parts)
        parts = []
        if ready(turn):
            parts.append(key_grads(turn))
        if ready(turn + 2):
            parts.append(weights(turn + 2))
        together(*parts)
    together(query_grads(GROUP - 1))

    for at in tiles:
        send_back(at).wait()
    for head in range(GROUP):
        send(att_all, att_ref, head, 0).wait()
        send(dq_all, dq_ref, head, 1).wait()


def attend(group, queries, d_out, far, keys_values, base, which, starts, near, keep, earlier):
    rows = queries.shape[1]
    keys = (REACH + 2) * rows
    whole = lambda shape: pl.BlockSpec(shape, lambda step: (0,) * len(shape))
    hbm = pl.BlockSpec(memory_space=pl.ANY)
    far_shape = (REACH, 2, rows, HEAD_SIZE)
    local_shape = (2, 2, rows, HEAD_SIZE)
    held = pltpu.VMEM((GROUP, 2, rows, HEAD_SIZE), jnp.bfloat16)
    flops = 6 * 2 * keys * 2 * rows * HEAD_SIZE * GROUP
    return pl.pallas_call(
        functools.partial(kernel, rows, group),
        grid=(1,),
        in_specs=[
            hbm,
            hbm,
            hbm,
            hbm,
            pl.BlockSpec(memory_space=pltpu.SMEM),
            pl.BlockSpec(memory_space=pltpu.SMEM),
            whole((1, 2 * rows)),
            whole((2 * rows, 2 * rows)),
            whole((1, 2 * rows)),
        ]
        + [hbm] * len(earlier),
        out_specs=[hbm, hbm, hbm, hbm],
        out_shape=[
            jax.ShapeDtypeStruct(queries.shape, jnp.bfloat16),
            jax.ShapeDtypeStruct(queries.shape, jnp.bfloat16),
            jax.ShapeDtypeStruct(far_shape, jnp.bfloat16),
            jax.ShapeDtypeStruct(local_shape, jnp.float32),
        ],
        scratch_shapes=[
            pltpu.VMEM((REACH + 2, rows, HEAD_SIZE), jnp.bfloat16),
            pltpu.VMEM((REACH + 2, rows, HEAD_SIZE), jnp.bfloat16),
            pltpu.VMEM((HEAD_SIZE, keys), jnp.bfloat16),
            pltpu.VMEM((HEAD_SIZE, keys), jnp.bfloat16),
            pltpu.VMEM((keys, 2 * rows), jnp.float32),
            pltpu.VMEM((2, keys, 2 * rows), jnp.float32),
            pltpu.VMEM((SLOTS, keys, 2 * rows), jnp.bfloat16),
            pltpu.VMEM((2, HEAD_SIZE, 2 * rows), jnp.bfloat16),
            pltpu.VMEM((2, 8, 2 * rows), jnp.float32),
            pltpu.VMEM((2, keys, 2 * rows), jnp.bfloat16),
            pltpu.VMEM((keys, HEAD_SIZE), jnp.float32),
            pltpu.VMEM((keys, HEAD_SIZE), jnp.float32),
            held,
            held,
            held,
            held,
            pltpu.VMEM(far_shape, jnp.bfloat16),
            pltpu.VMEM(local_shape, jnp.float32),
            pltpu.SemaphoreType.DMA((GROUP, 2)),
            pltpu.SemaphoreType.DMA((GROUP, 2)),
            pltpu.SemaphoreType.DMA((2, REACH)),
            pltpu.SemaphoreType.DMA((2,)),
            pltpu.SemaphoreType.DMA((keys // TILE,)),
        ],
        input_output_aliases={9 + i: i for i in range(len(earlier))},
        compiler_params=pltpu.CompilerParams(vmem_limit_bytes=VMEM_LIMIT),
        cost_estimate=pl.CostEstimate(
            flops=2 * flops, bytes_accessed=6 * 2**20, transcendentals=keys * 2 * rows * GROUP
        ),
        name=f"attend_{group}",
    )(queries, d_out, far, keys_values, base, which, starts, near, keep, *earlier)


def masks(doc_start, slab, place, places):
    rows = doc_start.shape[0]
    offset = jnp.arange(rows, dtype=jnp.int32)
    starts = jnp.concatenate([doc_start, doc_start])[None, :]
    slot = jnp.arange(REACH, dtype=jnp.int32)
    which = (slot >= place).astype(jnp.int32)
    base = rows * (places * (slab - which) + slot)
    same = doc_start[:, None] == starts
    k_blk = (offset // BLOCK)[:, None]
    q_blk = jnp.concatenate([offset // BLOCK] * 2)[None, :]
    noisy = (jnp.arange(2 * rows, dtype=jnp.int32) >= rows)[None, :]
    own_clean = same & (k_blk + noisy.astype(jnp.int32) <= q_blk)
    own_noisy = same & noisy & (k_blk == q_blk)
    near = jnp.where(jnp.concatenate([own_clean, own_noisy], 0), 0.0, NEGATIVE)
    return base, which, starts, near.astype(jnp.float32)


def local(queries, keys_values, d_out, doc_start, block_bits):
    rows = queries.shape[1]
    slabs, places = lax.axis_size("slab"), lax.axis_size("place")
    slab, place, head = (lax.axis_index(a) for a in ("slab", "place", "head"))
    kv_heads = keys_values.shape[3] // HEAD_SIZE
    later = [(i, i + 1) for i in range(slabs - 1)]
    sooner = [(i + 1, i) for i in range(slabs - 1)]
    slot = jnp.arange(places, dtype=jnp.int32)[:, None, None, None]
    after = slot > place

    own = keys_values[:, 0]
    before = lax.ppermute(own, "slab", later)
    far = []
    for group in range(kv_heads):
        part = slice(group * HEAD_SIZE, (group + 1) * HEAD_SIZE)
        if group == 0:
            send = jnp.where(after, own[None, :, :, part], before[None, :, :, part])
            far.append(lax.all_to_all(send, "place", 0, 0))
        else:
            send = jnp.stack([own[:, :, part], before[:, :, part]])
            far.append(lax.all_gather(send, "place"))

    other = lax.ppermute(block_bits, "head", [(0, 1), (1, 0)])
    bits = jnp.where(
        head == 0,
        jnp.concatenate([block_bits, other]),
        jnp.concatenate([other, block_bits]),
    )
    keep = jnp.concatenate([jnp.ones((rows,), jnp.int32), jnp.repeat(bits, BLOCK)])
    keep = keep.astype(jnp.float32)[None, :]
    base, which, starts, near = masks(doc_start, slab, place, places)

    earlier = ()
    totals, noisy = [], []
    for group in range(kv_heads):
        att, dq, back, mine = attend(
            group, queries, d_out, far[group], keys_values, base, which, starts, near, keep, earlier
        )
        earlier = (att, dq)
        if totals:
            back, totals[-1] = lax.optimization_barrier((back, totals[-1]))
        terms = lax.all_to_all(back, "place", 0, 0)
        totals.append(terms)
        noisy.append(mine)
    here, there = [], []
    for terms in totals:
        terms = terms.astype(jnp.float32)
        here.append(jnp.sum(jnp.where(after, terms, 0.0), 0))
        there.append(jnp.sum(jnp.where(after, 0.0, terms), 0).astype(jnp.bfloat16))
    arrived = lax.ppermute(jnp.concatenate(there, -1), "slab", sooner)
    clean = jnp.concatenate([a + b[:, 0] for a, b in zip(here, noisy)], -1)
    clean = clean + arrived.astype(jnp.float32)
    grad = jnp.stack([clean, jnp.concatenate([b[:, 1] for b in noisy], -1)], 1)
    return att, dq, grad.astype(jnp.bfloat16)


def solution(mesh):
    shards, heads = mesh.devices.shape
    cut = Mesh(mesh.devices.reshape(shards // REACH, REACH, heads), ("slab", "place", "head"))
    pos = ("slab", "place")
    in_specs = (
        P(None, pos, "head"),
        P(None, None, pos, "head"),
        P(None, pos, "head"),
        P(pos),
        P((*pos, "head")),
    )
    out_specs = (P(None, pos, "head"), P(None, pos, "head"), P(None, None, pos, "head"))
    return jax.shard_map(local, mesh=cut, in_specs=in_specs, out_specs=out_specs, check_vma=False)
```

```python
import functools
import math

import jax
import jax.numpy as jnp
from jax import lax
from jax.experimental import pallas as pl
from jax.experimental.pallas import tpu as pltpu
from jax.sharding import Mesh
from jax.sharding import PartitionSpec as P

BLOCK = 16
QUERY_HEADS = 32
KEY_VALUE_HEADS = 4
HEAD_SIZE = 128
GROUP = QUERY_HEADS // KEY_VALUE_HEADS
REACH = 16
NEGATIVE = -1e30
SCALE = 1.0 / math.sqrt(HEAD_SIZE)
SCALE_LOG2 = SCALE * math.log2(math.e)
TILE = 256
SLOTS = 3
VMEM_LIMIT = 50 * 2**20

NT = (((1,), (1,)), ((), ()))


def dot(a, b, dims=(((1,), (0,)), ((), ()))):
    return lax.dot_general(a, b, dims, preferred_element_type=jnp.float32)


def fold(x, op):
    return op(x.reshape(x.shape[0] // 8, 8, x.shape[1]), 0)


def kernel(
    rows,
    group,
    q_ref,
    do_ref,
    far_ref,
    own_ref,
    base_ref,
    starts_ref,
    near_ref,
    keep_ref,
    *rest,
):
    att_ref, dq_ref, back_ref, local_ref = rest[-27:-23]
    k_all, v_all, k_t, v_t, bias_all, s_all, p_all, g_all, delta_all, ds_all = rest[-23:-13]
    dk_all, dv_all, q_all, do_all, att_all, dq_all, back_all, local_all = rest[-13:-5]
    arrive, leave, arrive_far, arrive_own, leave_back = rest[-5:]
    keys = k_t.shape[1]
    per = TILE // rows
    tiles = [pl.ds(at, TILE) for at in range(0, keys, TILE)]
    own_columns = pl.ds(group * HEAD_SIZE, HEAD_SIZE)

    def tile_of(held, at):
        return held[pl.ds(at.start // rows, per)].reshape(TILE, HEAD_SIZE)

    def fetch_keys(i, held):
        return [
            pltpu.make_async_copy(far_ref.at[:, i], held.at[pl.ds(0, REACH)], arrive_far.at[i]),
            pltpu.make_async_copy(
                own_ref.at[i, :, :, own_columns], held.at[pl.ds(REACH, 2)], arrive_own.at[i]
            ),
        ]

    def send_back(at):
        slot = at.start // rows
        if slot < REACH:
            source, target = back_all.at[pl.ds(slot, per)], back_ref.at[pl.ds(slot, per)]
        else:
            source, target = local_all, local_ref
        return pltpu.make_async_copy(source, target, leave_back.at[slot // per])

    def columns(head):
        return pl.ds((group * GROUP + head) * HEAD_SIZE, HEAD_SIZE)

    def fetches(head):
        return [
            pltpu.make_async_copy(
                source.at[:, :, columns(head)], held.at[head], arrive.at[head, i]
            )
            for i, (source, held) in enumerate(((q_ref, q_all), (do_ref, do_all)))
        ]

    def send(held, target, head, i):
        return pltpu.make_async_copy(
            held.at[head], target.at[:, :, columns(head)], leave.at[head, i]
        )

    def rows_of(held, head):
        return held[head].reshape(2 * rows, HEAD_SIZE)

    def scores(head):
        for fetch in fetches(head):
            fetch.wait()
        q = rows_of(q_all, head)
        q_t = q.T
        top = jnp.full((8, 2 * rows), NEGATIVE, jnp.float32)
        for at in tiles:
            s = dot(tile_of(k_all, at), q_t) + bias_all[at, :]
            s_all[head % 2, at, :] = s
            top = jnp.maximum(top, fold(s, jnp.max))
            yield
        state[head] = jnp.max(top, 0, keepdims=True)

    def weights(head):
        top = state[head]
        total = jnp.zeros((8, 2 * rows), jnp.float32)
        for at in tiles:
            e = jnp.exp2((s_all[head % 2, at, :] - top) * SCALE_LOG2)
            p_all[head % SLOTS, at, :] = e.astype(jnp.bfloat16)
            total = total + fold(e, jnp.sum)
            yield
        state[head] = 1.0 / jnp.sum(total, 0, keepdims=True)

    def output(head):
        inverse = state[head]
        out_t = dot(v_t[...], p_all[head % SLOTS]) * inverse
        yield
        att_all[head] = out_t.T.astype(jnp.bfloat16).reshape(2, rows, HEAD_SIZE)
        send(att_all, att_ref, head, 0).start()
        yield
        out_t = out_t.astype(jnp.bfloat16).astype(jnp.float32)
        do_t = rows_of(do_all, head).astype(jnp.float32).T
        yield
        g_t = (do_t * (inverse * keep_ref[...])).astype(jnp.bfloat16)
        g_all[head % 2] = g_t
        delta = jnp.sum(g_t.astype(jnp.float32) * out_t, 0, keepdims=True)
        delta_all[head % 2] = jnp.broadcast_to(delta, (8, 2 * rows))
        yield

    def score_grads(head):
        g_t = g_all[head % 2]
        delta = delta_all[head % 2, 0:1, :]
        for at in tiles:
            dp = dot(tile_of(v_all, at), g_t)
            p = p_all[head % SLOTS, at, :].astype(jnp.float32)
            ds_all[head % 2, at, :] = (p * (dp - delta)).astype(jnp.bfloat16)
            yield

    def key_grads(head):
        q = rows_of(q_all, head)
        g = g_all[head % 2].T
        for at in tiles:
            dk = dot(ds_all[head % 2, at, :], q)
            dv = dot(p_all[head % SLOTS, at, :], g)
            if head > 0:
                dk = dk_all[at, :] + dk
                dv = dv_all[at, :] + dv
            if head < GROUP - 1:
                dk_all[at, :] = dk
                dv_all[at, :] = dv
            else:
                slot = at.start // rows
                for i, total in enumerate((dk * SCALE, dv)):
                    total = total.reshape(per, rows, HEAD_SIZE)
                    if slot < REACH:
                        back_all[pl.ds(slot, per), i] = total.astype(jnp.bfloat16)
                    else:
                        local_all[i] = total
                send_back(at).start()
            yield

    def query_grads(head):
        dq_t = dot(k_t[...], ds_all[head % 2]) * SCALE
        yield
        dq_all[head] = dq_t.T.astype(jnp.bfloat16).reshape(2, rows, HEAD_SIZE)
        send(dq_all, dq_ref, head, 1).start()
        yield

    def together(*parts):
        parts = list(parts)
        while parts:
            parts = [part for part in parts if next(part, part) is not part]

    def flip():
        for slot in range(REACH + 2):
            at = pl.ds(slot * rows, rows)
            k_t[:, at] = k_all[slot].T
            v_t[:, at] = v_all[slot].T
            if slot % per:
                yield

    for i, held in enumerate((k_all, v_all)):
        for fetch in fetch_keys(i, held):
            fetch.start()
        for fetch in fetches(i):
            fetch.start()
    for head in range(2, GROUP):
        for fetch in fetches(head):
            fetch.start()
    key = lax.broadcasted_iota(jnp.int32, (rows, 2 * rows), 0)
    starts = starts_ref[...]
    for slot in range(REACH):
        visible = key + base_ref[slot] >= starts
        bias_all[pl.ds(slot * rows, rows), :] = jnp.where(visible, 0.0, NEGATIVE)
    bias_all[pl.ds(REACH * rows, 2 * rows), :] = near_ref[...]
    for i, held in enumerate((k_all, v_all)):
        for fetch in fetch_keys(i, held):
            fetch.wait()

    state = {}
    for turn in range(-3, GROUP):
        ready = lambda head: 0 <= head < GROUP
        parts = []
        if ready(turn + 1):
            parts.append(output(turn + 1))
        if ready(turn):
            parts.append(score_grads(turn))
        if ready(turn + 3):
            parts.append(scores(turn + 3))
        if ready(turn - 1):
            parts.append(query_grads(turn - 1))
        if turn == -3:
            parts.append(flip())
        together(*parts)
        parts = []
        if ready(turn):
            parts.append(key_grads(turn))
        if ready(turn + 2):
            parts.append(weights(turn + 2))
        together(*parts)
    together(query_grads(GROUP - 1))

    for at in tiles:
        send_back(at).wait()
    for head in range(GROUP):
        send(att_all, att_ref, head, 0).wait()
        send(dq_all, dq_ref, head, 1).wait()


def attend(group, queries, d_out, far, keys_values, base, starts, near, keep, earlier):
    rows = queries.shape[1]
    keys = (REACH + 2) * rows
    whole = lambda shape: pl.BlockSpec(shape, lambda step: (0,) * len(shape))
    hbm = pl.BlockSpec(memory_space=pl.ANY)
    far_shape = (REACH, 2, rows, HEAD_SIZE)
    local_shape = (2, 2, rows, HEAD_SIZE)
    held = pltpu.VMEM((GROUP, 2, rows, HEAD_SIZE), jnp.bfloat16)
    flops = 6 * 2 * keys * 2 * rows * HEAD_SIZE * GROUP
    return pl.pallas_call(
        functools.partial(kernel, rows, group),
        grid=(1,),
        in_specs=[
            hbm,
            hbm,
            hbm,
            hbm,
            pl.BlockSpec(memory_space=pltpu.SMEM),
            whole((1, 2 * rows)),
            whole((2 * rows, 2 * rows)),
            whole((1, 2 * rows)),
        ]
        + [hbm] * len(earlier),
        out_specs=[hbm, hbm, hbm, hbm],
        out_shape=[
            jax.ShapeDtypeStruct(queries.shape, jnp.bfloat16),
            jax.ShapeDtypeStruct(queries.shape, jnp.bfloat16),
            jax.ShapeDtypeStruct(far_shape, jnp.bfloat16),
            jax.ShapeDtypeStruct(local_shape, jnp.float32),
        ],
        scratch_shapes=[
            pltpu.VMEM((REACH + 2, rows, HEAD_SIZE), jnp.bfloat16),
            pltpu.VMEM((REACH + 2, rows, HEAD_SIZE), jnp.bfloat16),
            pltpu.VMEM((HEAD_SIZE, keys), jnp.bfloat16),
            pltpu.VMEM((HEAD_SIZE, keys), jnp.bfloat16),
            pltpu.VMEM((keys, 2 * rows), jnp.float32),
            pltpu.VMEM((2, keys, 2 * rows), jnp.float32),
            pltpu.VMEM((SLOTS, keys, 2 * rows), jnp.bfloat16),
            pltpu.VMEM((2, HEAD_SIZE, 2 * rows), jnp.bfloat16),
            pltpu.VMEM((2, 8, 2 * rows), jnp.float32),
            pltpu.VMEM((2, keys, 2 * rows), jnp.bfloat16),
            pltpu.VMEM((keys, HEAD_SIZE), jnp.float32),
            pltpu.VMEM((keys, HEAD_SIZE), jnp.float32),
            held,
            held,
            held,
            held,
            pltpu.VMEM(far_shape, jnp.bfloat16),
            pltpu.VMEM(local_shape, jnp.float32),
            pltpu.SemaphoreType.DMA((GROUP, 2)),
            pltpu.SemaphoreType.DMA((GROUP, 2)),
            pltpu.SemaphoreType.DMA((2,)),
            pltpu.SemaphoreType.DMA((2,)),
            pltpu.SemaphoreType.DMA((keys // TILE,)),
        ],
        input_output_aliases={8 + i: i for i in range(len(earlier))},
        compiler_params=pltpu.CompilerParams(vmem_limit_bytes=VMEM_LIMIT),
        cost_estimate=pl.CostEstimate(
            flops=2 * flops, bytes_accessed=6 * 2**20, transcendentals=keys * 2 * rows * GROUP
        ),
        name=f"attend_{group}",
    )(queries, d_out, far, keys_values, base, starts, near, keep, *earlier)


def masks(doc_start, slab, place, places):
    rows = doc_start.shape[0]
    offset = jnp.arange(rows, dtype=jnp.int32)
    starts = jnp.concatenate([doc_start, doc_start])[None, :]
    slot = jnp.arange(REACH, dtype=jnp.int32)
    base = rows * (places * slab + slot - jnp.where(slot >= place, places, 0))
    same = doc_start[:, None] == starts
    k_blk = (offset // BLOCK)[:, None]
    q_blk = jnp.concatenate([offset // BLOCK] * 2)[None, :]
    noisy = (jnp.arange(2 * rows, dtype=jnp.int32) >= rows)[None, :]
    own_clean = same & (k_blk + noisy.astype(jnp.int32) <= q_blk)
    own_noisy = same & noisy & (k_blk == q_blk)
    near = jnp.where(jnp.concatenate([own_clean, own_noisy], 0), 0.0, NEGATIVE)
    return base, starts, near.astype(jnp.float32)


def local(queries, keys_values, d_out, doc_start, block_bits):
    rows = queries.shape[1]
    slabs, places = lax.axis_size("slab"), lax.axis_size("place")
    slab, place, head = (lax.axis_index(a) for a in ("slab", "place", "head"))
    kv_heads = keys_values.shape[3] // HEAD_SIZE
    later = [(i, i + 1) for i in range(slabs - 1)]
    sooner = [(i + 1, i) for i in range(slabs - 1)]
    slot = jnp.arange(places, dtype=jnp.int32)[:, None, None, None]
    after = slot > place

    own = keys_values[:, 0]
    before = lax.ppermute(own, "slab", later)
    far = []
    for group in range(kv_heads):
        part = slice(group * HEAD_SIZE, (group + 1) * HEAD_SIZE)
        send = jnp.where(after, own[None, :, :, part], before[None, :, :, part])
        far.append(lax.all_to_all(send, "place", 0, 0))

    other = lax.ppermute(block_bits, "head", [(0, 1), (1, 0)])
    bits = jnp.where(
        head == 0,
        jnp.concatenate([block_bits, other]),
        jnp.concatenate([other, block_bits]),
    )
    keep = jnp.concatenate([jnp.ones((rows,), jnp.int32), jnp.repeat(bits, BLOCK)])
    keep = keep.astype(jnp.float32)[None, :]
    base, starts, near = masks(doc_start, slab, place, places)

    earlier = ()
    totals, noisy = [], []
    for group in range(kv_heads):
        att, dq, back, mine = attend(
            group, queries, d_out, far[group], keys_values, base, starts, near, keep, earlier
        )
        earlier = (att, dq)
        if totals:
            back, totals[-1] = lax.optimization_barrier((back, totals[-1]))
        terms = lax.all_to_all(back, "place", 0, 0)
        totals.append(terms)
        noisy.append(mine)
    here, there = [], []
    for terms in totals:
        terms = terms.astype(jnp.float32)
        sums = (
            jnp.sum(jnp.where(after, terms, 0.0), 0),
            jnp.sum(jnp.where(after, 0.0, terms), 0).astype(jnp.bfloat16),
        )
        if len(here) < kv_heads - 1:
            sums = lax.optimization_barrier(sums)
        here.append(sums[0])
        there.append(sums[1])
    arrived = lax.ppermute(jnp.concatenate(there, -1), "slab", sooner)
    clean = jnp.concatenate([a + b[:, 0] for a, b in zip(here, noisy)], -1)
    clean = clean + arrived.astype(jnp.float32)
    grad = jnp.stack([clean, jnp.concatenate([b[:, 1] for b in noisy], -1)], 1)
    return att, dq, grad.astype(jnp.bfloat16)


def solution(mesh):
    shards, heads = mesh.devices.shape
    cut = Mesh(mesh.devices.reshape(shards // REACH, REACH, heads), ("slab", "place", "head"))
    pos = ("slab", "place")
    in_specs = (
        P(None, pos, "head"),
        P(None, None, pos, "head"),
        P(None, pos, "head"),
        P(pos),
        P((*pos, "head")),
    )
    out_specs = (P(None, pos, "head"), P(None, pos, "head"), P(None, None, pos, "head"))
    return jax.shard_map(local, mesh=cut, in_specs=in_specs, out_specs=out_specs, check_vma=False)
```

```python
import functools
import math

import jax
import jax.numpy as jnp
from jax import lax
from jax.experimental import pallas as pl
from jax.experimental.pallas import tpu as pltpu
from jax.sharding import Mesh
from jax.sharding import PartitionSpec as P

BLOCK = 16
QUERY_HEADS = 32
KEY_VALUE_HEADS = 4
HEAD_SIZE = 128
GROUP = QUERY_HEADS // KEY_VALUE_HEADS
REACH = 16
NEGATIVE = -1e30
SCALE = 1.0 / math.sqrt(HEAD_SIZE)
SCALE_LOG2 = SCALE * math.log2(math.e)
TILE = 256
SLOTS = 3
VMEM_LIMIT = 52 * 2**20

NT = (((1,), (1,)), ((), ()))


def dot(a, b, dims=(((1,), (0,)), ((), ()))):
    return lax.dot_general(a, b, dims, preferred_element_type=jnp.float32)


def fold(x, op):
    return op(x.reshape(x.shape[0] // 8, 8, x.shape[1]), 0)


def kernel(
    rows,
    group,
    q_ref,
    do_ref,
    far_ref,
    own_ref,
    base_ref,
    starts_ref,
    near_ref,
    keep_ref,
    *rest,
):
    att_ref, dq_ref, back_ref, local_ref = rest[-27:-23]
    k_all, v_all, k_t, v_t, bias_all, s_all, p_all, g_all, delta_all, ds_all = rest[-23:-13]
    dk_all, dv_all, q_all, do_all, att_all, dq_all, back_all, local_all = rest[-13:-5]
    arrive, leave, arrive_far, arrive_own, leave_back = rest[-5:]
    keys = k_t.shape[1]
    per = TILE // rows
    tiles = [pl.ds(at, TILE) for at in range(0, keys, TILE)]
    own_columns = pl.ds(group * HEAD_SIZE, HEAD_SIZE)

    def tile_of(held, at):
        return held[pl.ds(at.start // rows, per)].reshape(TILE, HEAD_SIZE)

    def fetch_keys(i, held):
        return [
            pltpu.make_async_copy(far_ref.at[:, i], held.at[pl.ds(0, REACH)], arrive_far.at[i]),
            pltpu.make_async_copy(
                own_ref.at[i, :, :, own_columns], held.at[pl.ds(REACH, 2)], arrive_own.at[i]
            ),
        ]

    def send_back(at):
        slot = at.start // rows
        if slot < REACH:
            source, target = back_all.at[pl.ds(slot, per)], back_ref.at[pl.ds(slot, per)]
        else:
            source, target = local_all, local_ref
        return pltpu.make_async_copy(source, target, leave_back.at[slot // per])

    def columns(head):
        return pl.ds((group * GROUP + head) * HEAD_SIZE, HEAD_SIZE)

    def fetches(head):
        return [
            pltpu.make_async_copy(
                source.at[:, :, columns(head)], held.at[head], arrive.at[head, i]
            )
            for i, (source, held) in enumerate(((q_ref, q_all), (do_ref, do_all)))
        ]

    def send(held, target, head, i):
        return pltpu.make_async_copy(
            held.at[head], target.at[:, :, columns(head)], leave.at[head, i]
        )

    def rows_of(held, head):
        return held[head].reshape(2 * rows, HEAD_SIZE)

    def scores(head):
        for fetch in fetches(head):
            fetch.wait()
        q = rows_of(q_all, head)
        q_t = q.T
        top = jnp.full((8, 2 * rows), NEGATIVE, jnp.float32)
        for at in tiles:
            s = dot(tile_of(k_all, at), q_t) + bias_all[at, :]
            s_all[head % 2, at, :] = s
            top = jnp.maximum(top, fold(s, jnp.max))
            yield
        state[head] = jnp.max(top, 0, keepdims=True)

    def weights(head):
        top = state[head]
        total = jnp.zeros((8, 2 * rows), jnp.float32)
        for at in tiles:
            e = jnp.exp2((s_all[head % 2, at, :] - top) * SCALE_LOG2)
            p_all[head % SLOTS, at, :] = e.astype(jnp.bfloat16)
            total = total + fold(e, jnp.sum)
            yield
        state[head] = 1.0 / jnp.sum(total, 0, keepdims=True)

    def output(head):
        inverse = state[head]
        out_t = dot(v_t[...], p_all[head % SLOTS]) * inverse
        yield
        att_all[head] = out_t.T.astype(jnp.bfloat16).reshape(2, rows, HEAD_SIZE)
        send(att_all, att_ref, head, 0).start()
        yield
        out_t = out_t.astype(jnp.bfloat16).astype(jnp.float32)
        do_t = rows_of(do_all, head).astype(jnp.float32).T
        yield
        g_t = (do_t * (inverse * keep_ref[...])).astype(jnp.bfloat16)
        g_all[head % 2] = g_t
        delta = jnp.sum(g_t.astype(jnp.float32) * out_t, 0, keepdims=True)
        delta_all[head % 2] = jnp.broadcast_to(delta, (8, 2 * rows))
        yield

    def score_grads(head):
        g_t = g_all[head % 2]
        delta = delta_all[head % 2, 0:1, :]
        for at in tiles:
            dp = dot(tile_of(v_all, at), g_t)
            p = p_all[head % SLOTS, at, :].astype(jnp.float32)
            ds_all[head % 2, at, :] = (p * (dp - delta)).astype(jnp.bfloat16)
            yield

    def key_grads(head):
        q = rows_of(q_all, head)
        g = g_all[head % 2].T
        for at in tiles:
            dk = dot(ds_all[head % 2, at, :], q)
            dv = dot(p_all[head % SLOTS, at, :], g)
            if head > 0:
                dk = dk_all[at, :] + dk
                dv = dv_all[at, :] + dv
            if head < GROUP - 1:
                dk_all[at, :] = dk
                dv_all[at, :] = dv
            else:
                slot = at.start // rows
                for i, total in enumerate((dk * SCALE, dv)):
                    total = total.reshape(per, rows, HEAD_SIZE)
                    if slot < REACH:
                        back_all[pl.ds(slot, per), i] = total.astype(jnp.bfloat16)
                    else:
                        local_all[i] = total
                send_back(at).start()
            yield

    def query_grads(head):
        dq_t = dot(k_t[...], ds_all[head % 2]) * SCALE
        yield
        dq_all[head] = dq_t.T.astype(jnp.bfloat16).reshape(2, rows, HEAD_SIZE)
        send(dq_all, dq_ref, head, 1).start()
        yield

    def together(*parts):
        parts = list(parts)
        while parts:
            parts = [part for part in parts if next(part, part) is not part]

    def flip():
        for slot in range(REACH + 2):
            at = pl.ds(slot * rows, rows)
            k_t[:, at] = k_all[slot].T
            v_t[:, at] = v_all[slot].T
            if slot % per:
                yield

    for i, held in enumerate((k_all, v_all)):
        for fetch in fetch_keys(i, held):
            fetch.start()
        for fetch in fetches(i):
            fetch.start()
    for head in range(2, GROUP):
        for fetch in fetches(head):
            fetch.start()
    key = lax.broadcasted_iota(jnp.int32, (rows, 2 * rows), 0)
    starts = starts_ref[...]
    for slot in range(REACH):
        visible = key + base_ref[slot] >= starts
        bias_all[pl.ds(slot * rows, rows), :] = jnp.where(visible, 0.0, NEGATIVE)
    bias_all[pl.ds(REACH * rows, 2 * rows), :] = near_ref[...]
    for i, held in enumerate((k_all, v_all)):
        for fetch in fetch_keys(i, held):
            fetch.wait()

    state = {}
    for turn in range(-3, GROUP):
        ready = lambda head: 0 <= head < GROUP
        parts = []
        if ready(turn + 1):
            parts.append(output(turn + 1))
        if ready(turn):
            parts.append(score_grads(turn))
        if ready(turn + 3):
            parts.append(scores(turn + 3))
        if ready(turn - 1):
            parts.append(query_grads(turn - 1))
        if turn == -3:
            parts.append(flip())
        together(*parts)
        parts = []
        if ready(turn):
            parts.append(key_grads(turn))
        if ready(turn + 2):
            parts.append(weights(turn + 2))
        together(*parts)
    together(query_grads(GROUP - 1))

    for at in tiles:
        send_back(at).wait()
    for head in range(GROUP):
        send(att_all, att_ref, head, 0).wait()
        send(dq_all, dq_ref, head, 1).wait()


def attend(group, queries, d_out, far, keys_values, base, starts, near, keep, earlier):
    rows = queries.shape[1]
    keys = (REACH + 2) * rows
    whole = lambda shape: pl.BlockSpec(shape, lambda step: (0,) * len(shape))
    hbm = pl.BlockSpec(memory_space=pl.ANY)
    far_shape = (REACH, 2, rows, HEAD_SIZE)
    local_shape = (2, 2, rows, HEAD_SIZE)
    held = pltpu.VMEM((GROUP, 2, rows, HEAD_SIZE), jnp.bfloat16)
    flops = 6 * 2 * keys * 2 * rows * HEAD_SIZE * GROUP
    return pl.pallas_call(
        functools.partial(kernel, rows, group),
        grid=(1,),
        in_specs=[
            hbm,
            hbm,
            hbm,
            hbm,
            pl.BlockSpec(memory_space=pltpu.SMEM),
            whole((1, 2 * rows)),
            whole((2 * rows, 2 * rows)),
            whole((1, 2 * rows)),
        ]
        + [hbm] * len(earlier),
        out_specs=[hbm, hbm, hbm, hbm],
        out_shape=[
            jax.ShapeDtypeStruct(queries.shape, jnp.bfloat16),
            jax.ShapeDtypeStruct(queries.shape, jnp.bfloat16),
            jax.ShapeDtypeStruct(far_shape, jnp.bfloat16),
            jax.ShapeDtypeStruct(local_shape, jnp.float32),
        ],
        scratch_shapes=[
            pltpu.VMEM((REACH + 2, rows, HEAD_SIZE), jnp.bfloat16),
            pltpu.VMEM((REACH + 2, rows, HEAD_SIZE), jnp.bfloat16),
            pltpu.VMEM((HEAD_SIZE, keys), jnp.bfloat16),
            pltpu.VMEM((HEAD_SIZE, keys), jnp.bfloat16),
            pltpu.VMEM((keys, 2 * rows), jnp.float32),
            pltpu.VMEM((2, keys, 2 * rows), jnp.float32),
            pltpu.VMEM((SLOTS, keys, 2 * rows), jnp.bfloat16),
            pltpu.VMEM((2, HEAD_SIZE, 2 * rows), jnp.bfloat16),
            pltpu.VMEM((2, 8, 2 * rows), jnp.float32),
            pltpu.VMEM((2, keys, 2 * rows), jnp.bfloat16),
            pltpu.VMEM((keys, HEAD_SIZE), jnp.float32),
            pltpu.VMEM((keys, HEAD_SIZE), jnp.float32),
            held,
            held,
            held,
            held,
            pltpu.VMEM(far_shape, jnp.bfloat16),
            pltpu.VMEM(local_shape, jnp.float32),
            pltpu.SemaphoreType.DMA((GROUP, 2)),
            pltpu.SemaphoreType.DMA((GROUP, 2)),
            pltpu.SemaphoreType.DMA((2,)),
            pltpu.SemaphoreType.DMA((2,)),
            pltpu.SemaphoreType.DMA((keys // TILE,)),
        ],
        input_output_aliases={8 + i: i for i in range(len(earlier))},
        compiler_params=pltpu.CompilerParams(vmem_limit_bytes=VMEM_LIMIT),
        cost_estimate=pl.CostEstimate(
            flops=2 * flops, bytes_accessed=6 * 2**20, transcendentals=keys * 2 * rows * GROUP
        ),
        name=f"attend_{group}",
    )(queries, d_out, far, keys_values, base, starts, near, keep, *earlier)


def settle_kernel(place_ref, terms_ref, mine_ref, here_ref, there_ref):
    for i in range(2):
        here = mine_ref[i, 0]
        there = jnp.zeros_like(here)
        for slot in range(REACH):
            term = terms_ref[slot, i].astype(jnp.float32)
            after = (slot > place_ref[0]).astype(jnp.float32)
            here = here + term * after
            there = there + term * (1.0 - after)
        here_ref[i] = here
        there_ref[i] = there.astype(jnp.bfloat16)


def settle(group, place, terms, mine):
    shape = terms.shape[1:]
    whole = lambda shape: pl.BlockSpec(shape, lambda: (0,) * len(shape))
    return pl.pallas_call(
        settle_kernel,
        in_specs=[pl.BlockSpec(memory_space=pltpu.SMEM), whole(terms.shape), whole(mine.shape)],
        out_specs=[whole(shape), whole(shape)],
        out_shape=[
            jax.ShapeDtypeStruct(shape, jnp.float32),
            jax.ShapeDtypeStruct(shape, jnp.bfloat16),
        ],
        compiler_params=pltpu.CompilerParams(vmem_limit_bytes=12 * 2**20),
        cost_estimate=pl.CostEstimate(
            flops=4 * terms.size, bytes_accessed=2 * terms.size, transcendentals=0
        ),
        name=f"settle_{group}",
    )(place[None], terms, mine)


def masks(doc_start, slab, place, places):
    rows = doc_start.shape[0]
    offset = jnp.arange(rows, dtype=jnp.int32)
    starts = jnp.concatenate([doc_start, doc_start])[None, :]
    slot = jnp.arange(REACH, dtype=jnp.int32)
    base = rows * (places * slab + slot - jnp.where(slot >= place, places, 0))
    same = doc_start[:, None] == starts
    k_blk = (offset // BLOCK)[:, None]
    q_blk = jnp.concatenate([offset // BLOCK] * 2)[None, :]
    noisy = (jnp.arange(2 * rows, dtype=jnp.int32) >= rows)[None, :]
    own_clean = same & (k_blk + noisy.astype(jnp.int32) <= q_blk)
    own_noisy = same & noisy & (k_blk == q_blk)
    near = jnp.where(jnp.concatenate([own_clean, own_noisy], 0), 0.0, NEGATIVE)
    return base, starts, near.astype(jnp.float32)


def local(queries, keys_values, d_out, doc_start, block_bits):
    rows = queries.shape[1]
    slabs, places = lax.axis_size("slab"), lax.axis_size("place")
    slab, place, head = (lax.axis_index(a) for a in ("slab", "place", "head"))
    kv_heads = keys_values.shape[3] // HEAD_SIZE
    later = [(i, i + 1) for i in range(slabs - 1)]
    sooner = [(i + 1, i) for i in range(slabs - 1)]
    slot = jnp.arange(places, dtype=jnp.int32)[:, None, None, None]
    after = slot > place

    own = keys_values[:, 0]
    before = lax.ppermute(own, "slab", later)
    far = []
    for group in range(kv_heads):
        part = slice(group * HEAD_SIZE, (group + 1) * HEAD_SIZE)
        send = jnp.where(after, own[None, :, :, part], before[None, :, :, part])
        far.append(lax.all_to_all(send, "place", 0, 0))

    other = lax.ppermute(block_bits, "head", [(0, 1), (1, 0)])
    bits = jnp.where(
        head == 0,
        jnp.concatenate([block_bits, other]),
        jnp.concatenate([other, block_bits]),
    )
    keep = jnp.concatenate([jnp.ones((rows,), jnp.int32), jnp.repeat(bits, BLOCK)])
    keep = keep.astype(jnp.float32)[None, :]
    base, starts, near = masks(doc_start, slab, place, places)

    earlier = ()
    totals, noisy = [], []
    for group in range(kv_heads):
        att, dq, back, mine = attend(
            group, queries, d_out, far[group], keys_values, base, starts, near, keep, earlier
        )
        earlier = (att, dq)
        if totals:
            back, totals[-1] = lax.optimization_barrier((back, totals[-1]))
        terms = lax.all_to_all(back, "place", 0, 0)
        totals.append(terms)
        noisy.append(mine)
    here, there = [], []
    for group, (terms, mine) in enumerate(zip(totals, noisy)):
        sums = settle(group, place, terms, mine)
        here.append(sums[0])
        there.append(sums[1])
    arrived = lax.ppermute(jnp.concatenate(there, -1), "slab", sooner)
    clean = jnp.concatenate(here, -1) + arrived.astype(jnp.float32)
    grad = jnp.stack([clean, jnp.concatenate([b[:, 1] for b in noisy], -1)], 1)
    return att, dq, grad.astype(jnp.bfloat16)


def solution(mesh):
    shards, heads = mesh.devices.shape
    cut = Mesh(mesh.devices.reshape(shards // REACH, REACH, heads), ("slab", "place", "head"))
    pos = ("slab", "place")
    in_specs = (
        P(None, pos, "head"),
        P(None, None, pos, "head"),
        P(None, pos, "head"),
        P(pos),
        P((*pos, "head")),
    )
    out_specs = (P(None, pos, "head"), P(None, pos, "head"), P(None, None, pos, "head"))
    return jax.shard_map(local, mesh=cut, in_specs=in_specs, out_specs=out_specs, check_vma=False)
```
